128 devices in a mesh: az: 16 (over z_hi, x, core), rad: 8 (over z_lo, y).
Axes of the slice: x: 4, y: 4, z: 4 (z_hi: 2, z_lo: 2; z = z_hi * 2 + z_lo), core: 2. Of those that a mesh axis runs over, the one named last changes fastest.
Arguments:
- conserved: float32 [5, 16, 128, 4096], P(None, None, 'rad', 'az'), as said below
- shift_cells: int32 [128], P('rad'), may hold values from 0 to 4095, as said below
- shift_frac: float32 [128], P('rad'), may hold values from 0 to 1
- boundary_offset: int32 [1], replicated, may hold values from 0 to 4095
Outputs:
- advected: float32 [5, 16, 128, 4096], P(None, None, 'rad', 'az')
The draws below stay inside these ranges and needn't reach their ends.
Inputs may be any that keep to these rules, and one draw needn't show every extreme that they name: The density and pressure of conserved lie between 0.5 and 2 and each velocity component is at most 0.8 in magnitude. `shift_cells`: both 0 and 4095 occur in every draw.
All inputs are finite; a program needn't handle non-finite values.
Results may differ from the reference program's by a relative error of at most 0.0003.
Values sent between devices are 32-bit elements; how exact they have to be, the bound alone decides.
No kernel may reach another device: no remote copies, remote signals or barrier semaphores. Data moves between devices by JAX's collectives and lax.ppermute only.
A program may use at most 448 MiB of HBM per device.

```python
import jax
import jax.numpy as jnp
from jax import lax

NZ = 16
NR = 128
NA = 4096


gamma_ratio = 5.0 / 3.0


def draw_conserved(key, part):
    subkeys = jax.random.split(key, 3)
    grid_shape = (NZ, NR, NA)
    density = 0.5 * jnp.exp(jax.random.uniform(subkeys[0], grid_shape, jnp.float32, 0.0, 1.3862944))
    velocity = jnp.clip(0.3 * jax.random.normal(subkeys[1], (3,) + grid_shape, jnp.float32), -0.8, 0.8)
    pressure = 0.5 * jnp.exp(jax.random.uniform(subkeys[2], grid_shape, jnp.float32, 0.0, 1.3862944))
    momentum = density[None] * velocity
    energy = pressure / (gamma_ratio - 1.0) + 0.5 * density * jnp.sum(velocity * velocity, axis=0)
    return jnp.concatenate([density[None], momentum, energy[None]], axis=0).astype(jnp.float32)


def draw_shift_cells(key, part):
    subkeys = jax.random.split(jax.random.fold_in(key, 11), 2)
    values = jax.random.randint(subkeys[0], (NR,), 0, NA, jnp.int32)
    places = jax.random.permutation(subkeys[1], NR)
    values = values.at[places[0]].set(NA - 1)
    return values.at[places[1]].set(0)


def block_levels(key, dims, shards, least, largest):
    loudness = 1.0
    for position, blocks in shards:
        steps = jax.random.uniform(jax.random.fold_in(jax.random.fold_in(key, 6), position), (blocks,), jnp.float32, least / len(shards), largest / len(shards))
        loudness = loudness * jnp.repeat(jnp.exp(steps), dims[position] // blocks).reshape((-1,) + (1,) * (len(dims) - 1 - position))
    return loudness


def setup_inputs(seed: int = 0) -> dict:
    arg_keys = jax.random.split(jax.random.key(seed), 5)
    conserved = draw_conserved(jax.random.fold_in(arg_keys[4], 71), 0)
    shift_cells = draw_shift_cells(jax.random.fold_in(arg_keys[4], 71), 0)
    shift_frac = jnp.clip(1.0 * jax.random.uniform(arg_keys[2], (NR,), jnp.float32) ** block_levels(arg_keys[2], (NR,), ((0, 8),), -0.2, 0.2), 0.0, 1.0)
    boundary_offset = jax.random.randint(arg_keys[3], (1,), 0, NA).astype(jnp.int32)
    return dict(conserved=conserved, shift_cells=shift_cells, shift_frac=shift_frac, boundary_offset=boundary_offset)


gamma_ratio = 5.0 / 3.0
step_ratio = 0.06
omega_rate = 1.0
shear_rate = 1.5

def to_primitive(cons_state):
    density = cons_state[0:1]
    velocity = cons_state[1:4] / density
    kinetic = 0.5 * lax.optimization_barrier(jnp.sum(cons_state[1:4] * velocity, axis=0, keepdims=True))
    pressure = (gamma_ratio - 1.0) * (cons_state[4:5] - kinetic)
    return jnp.concatenate([density, velocity, pressure], axis=0)

def to_conserved(prim_state):
    density = prim_state[0:1]
    momentum = density * prim_state[1:4]
    energy = prim_state[4:5] / (gamma_ratio - 1.0) + 0.5 * lax.optimization_barrier(jnp.sum(momentum * prim_state[1:4], axis=0, keepdims=True))
    return jnp.concatenate([density, momentum, energy], axis=0)

def euler_flux(prim_state, cons_state, normal):
    normal_speed = prim_state[normal]
    pressure = prim_state[4]
    pieces = []
    for component in range(5):
        term = cons_state[component] * normal_speed
        if component == normal:
            term = term + pressure
        if component == 4:
            term = term + pressure * normal_speed
        pieces.append(term)
    return jnp.stack(pieces)

def rusanov(left_face, right_face, normal):
    left_cons = to_conserved(left_face)
    right_cons = to_conserved(right_face)
    left_reach = jnp.abs(left_face[normal]) + jnp.sqrt(gamma_ratio * left_face[4] / left_face[0])
    right_reach = jnp.abs(right_face[normal]) + jnp.sqrt(gamma_ratio * right_face[4] / right_face[0])
    reach = jnp.maximum(left_reach, right_reach)
    averaged = 0.5 * (euler_flux(left_face, left_cons, normal) + euler_flux(right_face, right_cons, normal))
    return averaged - 0.5 * reach * (right_cons - left_cons)

def minmod(lower_diff, upper_diff):
    smaller = jnp.where(jnp.abs(lower_diff) < jnp.abs(upper_diff), lower_diff, upper_diff)
    return jnp.where(lower_diff * upper_diff > 0.0, smaller, jnp.zeros_like(smaller))

def face_states(prim_state, along, margin, count, higher):
    if higher:
        centre = lax.slice_in_dim(prim_state, margin - 1, margin + count + 1, axis=along)
        below_cells = lax.slice_in_dim(prim_state, margin - 2, margin + count, axis=along)
        above_cells = lax.slice_in_dim(prim_state, margin, margin + count + 2, axis=along)
        slopes = minmod(centre - below_cells, above_cells - centre)
        left_face = lax.slice_in_dim(centre + 0.5 * slopes, 0, count + 1, axis=along)
        right_face = lax.slice_in_dim(centre - 0.5 * slopes, 1, count + 2, axis=along)
    else:
        left_face = lax.slice_in_dim(prim_state, margin - 1, margin + count, axis=along)
        right_face = lax.slice_in_dim(prim_state, margin, margin + count + 1, axis=along)
    return (left_face, right_face)

def divergence(padded, margin, higher):
    row_count = padded.shape[2] - 2 * margin
    cell_count = padded.shape[3] - 2 * margin
    prim_rad = to_primitive(padded[:, :, :, margin:margin + cell_count])
    left_face, right_face = face_states(prim_rad, 2, margin, row_count, higher)
    face_flux = rusanov(left_face, right_face, 1)
    summed = face_flux[:, :, 1:] - face_flux[:, :, :-1]
    prim_az = to_primitive(padded[:, :, margin:margin + row_count, :])
    left_face, right_face = face_states(prim_az, 3, margin, cell_count, higher)
    face_flux = rusanov(left_face, right_face, 2)
    summed = summed + (face_flux[:, :, :, 1:] - face_flux[:, :, :, :-1])
    interior = prim_az[:, :, :, margin:margin + cell_count]
    if higher:
        slopes = minmod(interior - jnp.roll(interior, 1, axis=1), jnp.roll(interior, -1, axis=1) - interior)
        left_face = jnp.roll(interior + 0.5 * slopes, 1, axis=1)
        right_face = interior - 0.5 * slopes
    else:
        left_face = jnp.roll(interior, 1, axis=1)
        right_face = interior
    face_flux = rusanov(left_face, right_face, 3)
    return summed + (jnp.roll(face_flux, -1, axis=1) - face_flux)

def sources(cons_state):
    nothing = jnp.zeros_like(cons_state[0])
    return jnp.stack([nothing, 2.0 * omega_rate * cons_state[2], -(2.0 - shear_rate) * omega_rate * cons_state[1], nothing, shear_rate * omega_rate * cons_state[1] * cons_state[2] / cons_state[0]])

def predictor(conserved, padded_one):
    summed = divergence(padded_one, 1, False)
    return conserved + 0.5 * step_ratio * (sources(conserved) - summed)

def corrector(conserved, half_state, padded_two):
    summed = divergence(padded_two, 2, True)
    return conserved + step_ratio * (sources(half_state) - summed)

def pad_global(fields, margin, offset):
    lower_rim = jnp.roll(fields[:, :, -margin:, :], offset, axis=3)
    upper_rim = jnp.roll(fields[:, :, :margin, :], -offset, axis=3)
    stacked = jnp.concatenate([lower_rim, fields, upper_rim], axis=2)
    return jnp.concatenate([stacked[:, :, :, -margin:], stacked, stacked[:, :, :, :margin]], axis=3)

def orbital_remap(updated, shift_cells, shift_frac):

    def one_row(column, whole_shift, fraction):
        shifted = jnp.roll(column, whole_shift, axis=2)
        return (1.0 - fraction) * shifted + fraction * jnp.roll(shifted, 1, axis=2)
    return jax.vmap(one_row, in_axes=(2, 0, 0), out_axes=2)(updated, shift_cells, shift_frac)

def reference(conserved, shift_cells, shift_frac, boundary_offset):
    offset = boundary_offset[0]
    half_state = predictor(conserved, pad_global(conserved, 1, offset))
    updated = corrector(conserved, half_state, pad_global(half_state, 2, offset))
    return orbital_remap(updated, shift_cells, shift_frac)
```

```python
import functools

import jax
import jax.numpy as jnp
from jax import lax
from jax.experimental import pallas as pl
from jax.experimental.pallas import tpu as pltpu
from jax.sharding import PartitionSpec as P

gamma_ratio = 5.0 / 3.0
step_ratio = 0.06
omega_rate = 1.0
shear_rate = 1.5

NZ = 16
NROW = 16
NC = 256
LANES = 128
WIDTH = 3
NFULL = NROW + 2 * WIDTH
GROUP = 8
VMEM = pl.BlockSpec(memory_space=pltpu.VMEM)
SMEM = pl.BlockSpec(memory_space=pltpu.SMEM)
PARAMS = pltpu.CompilerParams(vmem_limit_bytes=48 * 2**20)


def lanes_of(shape):
    return lax.broadcasted_iota(jnp.int32, shape, len(shape) - 1)


def reciprocal(x):
    guess = pl.reciprocal(x, approx=True)
    return guess * (2.0 - x * guess)


def primitive(cons):
    inverse = reciprocal(cons[0])
    vel = [cons[n] * inverse for n in (1, 2, 3)]
    kinetic = 0.5 * (cons[1] * vel[0] + cons[2] * vel[1] + cons[3] * vel[2])
    return [cons[0], *vel, (gamma_ratio - 1.0) * (cons[4] - kinetic)]


def conserved_of(prim):
    mom = [prim[0] * prim[n] for n in (1, 2, 3)]
    kinetic = 0.5 * (mom[0] * prim[1] + mom[1] * prim[2] + mom[2] * prim[3])
    return [prim[0], *mom, prim[4] * (1.0 / (gamma_ratio - 1.0)) + kinetic]


def sound(prim):
    scaled = gamma_ratio * prim[4]
    return scaled * lax.rsqrt(scaled * prim[0])


def flux_of(prim, cons, normal):
    speed = prim[normal]
    flux = [cons[normal]]
    for n in (1, 2, 3):
        term = cons[n] * speed
        flux.append(term + prim[4] if n == normal else term)
    flux.append((cons[4] + prim[4]) * speed)
    return flux


def twice_face(low_flux, low_cons, low_reach, flux, cons, reach):
    top = jnp.maximum(low_reach, reach)
    return [(a + b) - top * (v - u) for a, b, u, v in zip(low_flux, flux, low_cons, cons)]


def minmod(a, b):
    return jnp.maximum(jnp.minimum(a, b), 0.0) + jnp.minimum(jnp.maximum(a, b), 0.0)


def rolled(arrays, by, axis):
    return [pltpu.roll(x, by % x.shape[axis], axis) for x in arrays]


def first_order_faces(prim, cons, speed_of_sound, normal, axis):
    flux = flux_of(prim, cons, normal)
    reach = jnp.abs(prim[normal]) + speed_of_sound
    low_cons = rolled(cons, 1, axis)
    low_flux = [low_cons[normal], *rolled(flux[1:], 1, axis)]
    low_reach = pltpu.roll(reach, 1, axis)
    return twice_face(low_flux, low_cons, low_reach, flux, cons, reach)


def state_at(prim, normal):
    cons = conserved_of(prim)
    return flux_of(prim, cons, normal), cons, jnp.abs(prim[normal]) + sound(prim)


def second_order_faces(prim, normal, axis):
    diff = [x - y for x, y in zip(prim, rolled(prim, 1, axis))]
    half_slope = [0.5 * minmod(a, b) for a, b in zip(diff, rolled(diff, -1, axis))]
    low = rolled([x + s for x, s in zip(prim, half_slope)], 1, axis)
    high = [x - s for x, s in zip(prim, half_slope)]
    return twice_face(*state_at(low, normal), *state_at(high, normal))


def added_sources(cons, prim):
    return {
        1: 2.0 * omega_rate * cons[2],
        2: -(2.0 - shear_rate) * omega_rate * cons[1],
        4: shear_rate * omega_rate * cons[1] * prim[2],
    }


def row_of(ref, *index):
    return [ref[(*index, pl.ds(c * NZ, NZ), slice(None))] for c in range(5)]


def put_row(ref, index, arrays):
    for c in range(5):
        ref[index, pl.ds(c * NZ, NZ), :] = arrays[c]


def prep_kernel(rem_ref, x_ref, xt_ref, lo_ref, hi_ref, edge_ref):
    for c in range(5):
        xt_ref[:, pl.ds(c * NZ, NZ), :] = jnp.swapaxes(x_ref[pl.ds(c * NZ, NZ)], 0, 1)
    lo_ref[...] = xt_ref[:WIDTH]
    hi_ref[...] = xt_ref[NROW - WIDTH :]
    at_low = rem_ref[1] == 0
    first = jnp.where(at_low, 0, NROW - WIDTH)
    by = jnp.where(at_low, (NC - rem_ref[0]) % NC, rem_ref[0])
    for w in range(WIDTH):
        edge_ref[w] = pltpu.roll(xt_ref[first + w], by, 1)


def gather_kernel(rem_ref, xt_ref, up_ref, dn_ref, e1_ref, e2_ref, full_ref, strip_ref):
    rem, rad, last = rem_ref[0], rem_ref[1], rem_ref[2]
    full_ref[pl.ds(WIDTH, NROW)] = xt_ref[...]
    lane = lanes_of((WIDTH, 5 * NZ, NC))

    @pl.when(rad != 0)
    def _():
        full_ref[pl.ds(0, WIDTH)] = up_ref[...]

    @pl.when(rad == 0)
    def _():
        full_ref[pl.ds(0, WIDTH)] = jnp.where(lane >= rem, e1_ref[...], e2_ref[...])

    @pl.when(rad != last)
    def _():
        full_ref[pl.ds(NROW + WIDTH, WIDTH)] = dn_ref[...]

    @pl.when(rad == last)
    def _():
        full_ref[pl.ds(NROW + WIDTH, WIDTH)] = jnp.where(lane < NC - rem, e1_ref[...], e2_ref[...])

    group = lanes_of((5 * NZ, LANES)) // GROUP
    for tile, rows in enumerate((range(WIDTH, WIDTH + NROW), (0, 1, 2, NROW + 3, NROW + 4, NROW + 5))):
        packed = jnp.zeros((5 * NZ, LANES), jnp.float32)
        for g, row in enumerate(rows):
            moved = pltpu.roll(full_ref[row], g * GROUP + GROUP // 2, 1)[:, :LANES]
            packed = jnp.where(group == g, moved, packed)
        strip_ref[:, tile * LANES : (tile + 1) * LANES] = packed


def step_kernel(full_ref, own_ref, left_ref, right_ref, out_ref, prim_ref, half_ref, faces_ref, prev_ref, edge_ref):
    lane = lanes_of((NZ, NC))
    tile_lane = lanes_of((NZ, LANES))
    from_low = (tile_lane % GROUP) < GROUP // 2
    pred = 0.25 * step_ratio
    corr = 0.5 * step_ratio

    def edges(c, tile):
        rows, cols = pl.ds(c * NZ, NZ), pl.ds(tile * LANES, LANES)
        own = own_ref[rows, cols]
        low = jnp.where(from_low, left_ref[rows, cols], own)
        high = jnp.where(from_low, own, right_ref[rows, cols])
        return jnp.concatenate([low, high], axis=1)

    def keep_faces(which, tile, faces):
        for c in range(5):
            for side in range(2):
                faces_ref[which, side, pl.ds(c * NZ, NZ), :] = faces[c][:, side * LANES : (side + 1) * LANES]

    def patched(faces, which, group, count):
        lower, upper = [], []
        for c in range(5):
            rows = pl.ds(c * NZ, NZ)
            left = pltpu.roll(faces_ref[which, 0, rows, :], (2 * LANES - GROUP * group - GROUP // 2) % LANES, 1)
            tiles = [jnp.where(tile_lane < count, left, faces[c][:, :LANES]), faces[c][:, LANES:]]
            right = faces_ref[which, 1, rows, :]
            beyond = pltpu.roll(right, (2 * LANES - 1 - GROUP * group - GROUP // 2) % LANES, 1)
            if count > 1:
                inside = pltpu.roll(right, (2 * LANES - GROUP * group - GROUP // 2) % LANES, 1)
                tiles[1] = jnp.where(tile_lane == LANES - 1, inside, tiles[1])
            whole = jnp.concatenate(tiles, axis=1)
            lower.append(whole)
            above = pltpu.roll(whole, NC - 1, 1)
            upper.append(
                jnp.concatenate(
                    [above[:, :LANES], jnp.where(tile_lane == LANES - 1, beyond, above[:, LANES:])], axis=1
                )
            )
        return lower, upper

    ghost = [edges(c, 1) for c in range(5)]
    ghost_prim = primitive(ghost)
    keep_faces(1, 1, first_order_faces(ghost_prim, ghost, sound(ghost_prim), 2, 1))
    cons = [edges(c, 0) for c in range(5)]
    prim = primitive(cons)
    speed = sound(prim)
    az = first_order_faces(prim, cons, speed, 2, 1)
    keep_faces(0, 0, az)
    vert = first_order_faces(prim, cons, speed, 3, 0)
    in_tile = lane % LANES
    below = [
        jnp.where(in_tile < GROUP, a, b) for a, b in zip(rolled(ghost, -2 * GROUP, 1), rolled(cons, GROUP, 1))
    ]
    above = [
        jnp.where(in_tile >= LANES - GROUP, a, b)
        for a, b in zip(rolled(ghost, LANES - 4 * GROUP, 1), rolled(cons, -GROUP, 1))
    ]

    def rad_state(u):
        q = primitive(u)
        return flux_of(q, u, 1), u, jnp.abs(q[1]) + sound(q)

    mid_state = (flux_of(prim, cons, 1), cons, jnp.abs(prim[1]) + speed)
    rad_low = twice_face(*rad_state(below), *mid_state)
    rad_high = twice_face(*mid_state, *rad_state(above))
    source = added_sources(cons, prim)
    half = []
    for c in range(5):
        total = (rad_high[c] - rad_low[c]) + (pltpu.roll(az[c], NC - 1, 1) - az[c])
        total = total + (pltpu.roll(vert[c], NZ - 1, 0) - vert[c])
        value = cons[c] - pred * total
        half.append(value + 0.5 * step_ratio * source[c] if c in source else value)
    az = second_order_faces(primitive(half), 2, 1)
    for c in range(5):
        for side in range(2):
            edge_ref[side, pl.ds(c * NZ, NZ), :] = az[c][:, side * LANES : (side + 1) * LANES]

    def predict(i, carry):
        cons = row_of(full_ref, i)
        prim = primitive(cons)
        speed = sound(prim)
        flux = flux_of(prim, cons, 1)
        reach = jnp.abs(prim[1]) + speed

        @pl.when(i > 0)
        def _():
            low_cons = row_of(full_ref, i - 1)
            low_flux = row_of(prev_ref, 0)
            low_reach = prev_ref[1, pl.ds(0, NZ), :]
            rad = twice_face(low_flux, low_cons, low_reach, flux, cons, reach)

            @pl.when(i > 1)
            def _():
                done = [x - pred * y for x, y in zip(row_of(half_ref, 0), rad)]
                put_row(prim_ref, i - 1, primitive(done))

            @pl.when(i < NFULL - 1)
            def _():
                interior = jnp.logical_and(i >= WIDTH, i < WIDTH + NROW)
                which = jnp.where(interior, 0, 1)
                group = jnp.where(interior, i - WIDTH, jnp.where(i < WIDTH, i, i - NROW))
                lower, upper = patched(first_order_faces(prim, cons, speed, 2, 1), which, group, 1)
                vert = first_order_faces(prim, cons, speed, 3, 0)
                source = added_sources(cons, prim)
                for c in range(5):
                    total = (upper[c] - lower[c]) + (pltpu.roll(vert[c], NZ - 1, 0) - vert[c]) - rad[c]
                    value = cons[c] - pred * total
                    if c in source:
                        value = value + 0.5 * step_ratio * source[c]
                    half_ref[0, pl.ds(c * NZ, NZ), :] = value

        put_row(prev_ref, 0, flux)
        prev_ref[1, pl.ds(0, NZ), :] = reach
        return carry

    lax.fori_loop(0, NFULL, predict, 0)

    faces_ref[0] = edge_ref[...]

    def correct(i, carry):
        prim = row_of(prim_ref, i)
        half_slope = [
            0.5 * minmod(x - a, b - x) for x, a, b in zip(prim, row_of(prim_ref, i - 1), row_of(prim_ref, i + 1))
        ]
        high = [x - s for x, s in zip(prim, half_slope)]

        @pl.when(i > WIDTH - 1)
        def _():
            rad = twice_face(*state_at(row_of(prev_ref, 0), 1), *state_at(high, 1))

            @pl.when(i > WIDTH)
            def _():
                for c in range(5):
                    out_ref[i - WIDTH - 1, pl.ds(c * NZ, NZ), :] = half_ref[0, pl.ds(c * NZ, NZ), :] - corr * rad[c]

            @pl.when(i < WIDTH + NROW)
            def _():
                lower, upper = patched(second_order_faces(prim, 2, 1), 0, i - WIDTH, 2)
                vert = second_order_faces(prim, 3, 0)
                source = added_sources(conserved_of(prim), prim)
                for c in range(5):
                    total = (upper[c] - lower[c]) + (pltpu.roll(vert[c], NZ - 1, 0) - vert[c]) - rad[c]
                    value = full_ref[i, pl.ds(c * NZ, NZ), :] - corr * total
                    if c in source:
                        value = value + step_ratio * source[c]
                    half_ref[0, pl.ds(c * NZ, NZ), :] = value

        put_row(prev_ref, 0, [x + s for x, s in zip(prim, half_slope)])
        return carry

    lax.fori_loop(WIDTH - 1, WIDTH + NROW + 1, correct, 0)


def remap_kernel(count, shift_ref, frac_ref, x_ref, o_ref, held_ref):
    row = shift_ref[NROW]
    shift, frac = shift_ref[row], frac_ref[row]
    hop = jnp.bitwise_and(jnp.right_shift(shift, 8), count - 1)
    rem = jnp.bitwise_and(shift, NC - 1)
    lane = lanes_of((5 * NZ, NC))

    def one(m, carry):
        here = jnp.bitwise_and(m + count - 1, count - 1)
        before = jnp.bitwise_and(m + count - 2, count - 1)
        block = x_ref[here]
        lower = jnp.where(lane == 0, pltpu.roll(x_ref[before], 1, 1), pltpu.roll(block, 1, 1))
        moved = pltpu.roll((1.0 - frac) * block + frac * lower, rem, 1)

        @pl.when(m > 0)
        def _():
            o_ref[jnp.bitwise_and(m + hop + count - 1, count - 1)] = jnp.where(lane >= rem, moved, held_ref[...])

        held_ref[...] = moved
        return carry

    lax.fori_loop(0, count + 1, one, 0)


def finish_kernel(y_ref, o_ref):
    for c in range(5):
        o_ref[pl.ds(c * NZ, NZ)] = jnp.swapaxes(y_ref[:, pl.ds(c * NZ, NZ), :], 0, 1)


def shape(*dims):
    return jax.ShapeDtypeStruct(dims, jnp.float32)


def local(conserved, shift_cells, shift_frac, boundary_offset):
    azs, rads = lax.axis_size("az"), lax.axis_size("rad")
    az, rad = lax.axis_index("az"), lax.axis_index("rad")
    offset = boundary_offset[0]
    hop, rem = offset // NC, offset % NC
    scalars = jnp.stack([rem, rad, jnp.int32(rads - 1)]).astype(jnp.int32)
    rim = shape(WIDTH, 5 * NZ, NC)
    rows, lo, hi, edge = pl.pallas_call(
        prep_kernel,
        out_shape=(shape(NROW, 5 * NZ, NC), rim, rim, rim),
        in_specs=[SMEM, VMEM],
        out_specs=(VMEM,) * 4,
        compiler_params=PARAMS,
    )(scalars, conserved.reshape(5 * NZ, NROW, NC))

    from_below = lax.ppermute(hi, "rad", [(i, i + 1) for i in range(rads - 1)])
    from_above = lax.ppermute(lo, "rad", [(i + 1, i) for i in range(rads - 1)])

    def ends(k):
        pairs = [(a * rads + rads - 1, (a + k) % azs * rads) for a in range(azs)]
        return pairs + [(b, a) for a, b in pairs]

    def moved_by(k):
        def send(block):
            return tuple(lax.ppermute(block, ("az", "rad"), ends(j % azs)) for j in (k, k + 1))

        return send

    first, second = lax.switch(hop, [moved_by(k) for k in range(azs)], edge)
    full, strip = pl.pallas_call(
        gather_kernel,
        out_shape=(shape(NFULL, 5 * NZ, NC), shape(5 * NZ, 2 * LANES)),
        in_specs=[SMEM] + [VMEM] * 5,
        out_specs=(VMEM,) * 2,
        compiler_params=PARAMS,
    )(scalars, rows, from_below, from_above, first, second)
    left = lax.ppermute(strip, "az", [(i, (i + 1) % azs) for i in range(azs)])
    right = lax.ppermute(strip, "az", [((i + 1) % azs, i) for i in range(azs)])
    updated = pl.pallas_call(
        step_kernel,
        out_shape=shape(NROW, 5 * NZ, NC),
        in_specs=[VMEM] * 4,
        out_specs=VMEM,
        scratch_shapes=[
            pltpu.VMEM((NFULL, 5 * NZ, NC), jnp.float32),
            pltpu.VMEM((1, 5 * NZ, NC), jnp.float32),
            pltpu.VMEM((2, 2, 5 * NZ, LANES), jnp.float32),
            pltpu.VMEM((2, 5 * NZ, NC), jnp.float32),
            pltpu.VMEM((2, 5 * NZ, LANES), jnp.float32),
        ],
        compiler_params=PARAMS,
    )(full, strip, left, right)

    whole_row = lax.all_to_all(updated, "az", 0, 0, tiled=True)
    shifts = jnp.concatenate([shift_cells, az[None].astype(jnp.int32)])
    moved = pl.pallas_call(
        functools.partial(remap_kernel, azs),
        out_shape=shape(azs, 5 * NZ, NC),
        in_specs=[SMEM, SMEM, VMEM],
        out_specs=VMEM,
        scratch_shapes=[pltpu.VMEM((5 * NZ, NC), jnp.float32)],
        compiler_params=PARAMS,
    )(shifts, shift_frac, whole_row)
    back = lax.all_to_all(moved, "az", 0, 0, tiled=True)
    result = pl.pallas_call(
        finish_kernel,
        out_shape=shape(5 * NZ, NROW, NC),
        in_specs=[VMEM],
        out_specs=VMEM,
        compiler_params=PARAMS,
    )(back)
    return result.reshape(5, NZ, NROW, NC)


def solution(mesh):
    in_specs = (P(None, None, "rad", "az"), P("rad"), P("rad"), P())
    out_specs = P(None, None, "rad", "az")
    return jax.shard_map(local, mesh=mesh, in_specs=in_specs, out_specs=out_specs, check_vma=False)
```

```python
import functools

import jax
import jax.numpy as jnp
from jax import lax
from jax.experimental import pallas as pl
from jax.experimental.pallas import tpu as pltpu
from jax.sharding import PartitionSpec as P

gamma_ratio = 5.0 / 3.0
step_ratio = 0.06
omega_rate = 1.0
shear_rate = 1.5

NZ = 16
NROW = 16
NC = 256
LANES = 128
WIDTH = 3
PRED = 0.25 * step_ratio
CORR = 0.5 * step_ratio
GROUP = 8
VMEM = pl.BlockSpec(memory_space=pltpu.VMEM)
SMEM = pl.BlockSpec(memory_space=pltpu.SMEM)
PARAMS = pltpu.CompilerParams(vmem_limit_bytes=48 * 2**20)


def lanes_of(shape):
    return lax.broadcasted_iota(jnp.int32, shape, len(shape) - 1)


def reciprocal(x):
    guess = pl.reciprocal(x, approx=True)
    return guess * (2.0 - x * guess)


def primitive(cons):
    inverse = reciprocal(cons[0])
    vel = [cons[n] * inverse for n in (1, 2, 3)]
    kinetic = 0.5 * (cons[1] * vel[0] + cons[2] * vel[1] + cons[3] * vel[2])
    return [cons[0], *vel, (gamma_ratio - 1.0) * (cons[4] - kinetic)]


def conserved_of(prim):
    mom = [prim[0] * prim[n] for n in (1, 2, 3)]
    kinetic = 0.5 * (mom[0] * prim[1] + mom[1] * prim[2] + mom[2] * prim[3])
    return [prim[0], *mom, prim[4] * (1.0 / (gamma_ratio - 1.0)) + kinetic]


def sound(prim):
    scaled = gamma_ratio * prim[4]
    return scaled * lax.rsqrt(scaled * prim[0])


def flux_of(prim, cons, normal):
    speed = prim[normal]
    flux = [cons[normal]]
    for n in (1, 2, 3):
        term = cons[n] * speed
        flux.append(term + prim[4] if n == normal else term)
    flux.append((cons[4] + prim[4]) * speed)
    return flux


def twice_face(low_flux, low_cons, low_reach, flux, cons, reach):
    top = jnp.maximum(low_reach, reach)
    return [(a + b) - top * (v - u) for a, b, u, v in zip(low_flux, flux, low_cons, cons)]


def minmod(a, b):
    return jnp.maximum(jnp.minimum(a, b), 0.0) + jnp.minimum(jnp.maximum(a, b), 0.0)


def rolled(arrays, by, axis):
    return [pltpu.roll(x, by % x.shape[axis], axis) for x in arrays]


def first_order_faces(prim, cons, speed_of_sound, normal, axis):
    flux = flux_of(prim, cons, normal)
    reach = jnp.abs(prim[normal]) + speed_of_sound
    low_cons = rolled(cons, 1, axis)
    low_flux = [low_cons[normal], *rolled(flux[1:], 1, axis)]
    low_reach = pltpu.roll(reach, 1, axis)
    return twice_face(low_flux, low_cons, low_reach, flux, cons, reach)


def state_at(prim, normal):
    cons = conserved_of(prim)
    return flux_of(prim, cons, normal), cons, jnp.abs(prim[normal]) + sound(prim)


def second_order_faces(prim, normal, axis):
    diff = [x - y for x, y in zip(prim, rolled(prim, 1, axis))]
    half_slope = [0.5 * minmod(a, b) for a, b in zip(diff, rolled(diff, -1, axis))]
    low = rolled([x + s for x, s in zip(prim, half_slope)], 1, axis)
    high = [x - s for x, s in zip(prim, half_slope)]
    return twice_face(*state_at(low, normal), *state_at(high, normal))


def added_sources(cons, prim):
    return {
        1: 2.0 * omega_rate * cons[2],
        2: -(2.0 - shear_rate) * omega_rate * cons[1],
        4: shear_rate * omega_rate * cons[1] * prim[2],
    }


def row_of(ref, *index):
    return [ref[(*index, pl.ds(c * NZ, NZ), slice(None))] for c in range(5)]


def put_row(ref, index, arrays):
    for c in range(5):
        ref[index, pl.ds(c * NZ, NZ), :] = arrays[c]


def tile_lanes():
    return lanes_of((NZ, LANES))


def edge_faces_of(strip):
    prim = primitive(strip)
    speed = sound(prim)
    return prim, speed, first_order_faces(prim, strip, speed, 2, 1)


def keep_faces(ref, faces):
    for c in range(5):
        for side in range(2):
            ref[side, pl.ds(c * NZ, NZ), :] = faces[c][:, side * LANES : (side + 1) * LANES]


def strip_half(cons, prim, speed, az, below, above):
    def rad_state(u):
        q = primitive(u)
        return flux_of(q, u, 1), u, jnp.abs(q[1]) + sound(q)

    mid_state = (flux_of(prim, cons, 1), cons, jnp.abs(prim[1]) + speed)
    rad_low = twice_face(*rad_state(below), *mid_state)
    rad_high = twice_face(*mid_state, *rad_state(above))
    vert = first_order_faces(prim, cons, speed, 3, 0)
    source = added_sources(cons, prim)
    half = []
    for c in range(5):
        total = (rad_high[c] - rad_low[c]) + (pltpu.roll(az[c], NC - 1, 1) - az[c])
        total = total + (pltpu.roll(vert[c], NZ - 1, 0) - vert[c])
        value = cons[c] - PRED * total
        half.append(value + 0.5 * step_ratio * source[c] if c in source else value)
    return half


def patched(faces, faces_ref, group, count):
    lane = tile_lanes()
    lower, upper = [], []
    for c in range(5):
        rows = pl.ds(c * NZ, NZ)
        at_edge = (2 * LANES - GROUP * group - GROUP // 2) % LANES
        before_edge = (3 * LANES - 1 - GROUP * group - GROUP // 2) % LANES
        left = pltpu.roll(faces_ref[0, rows, :], at_edge, 1)
        tiles = [jnp.where(lane < count, left, faces[c][:, :LANES]), faces[c][:, LANES:]]
        right = faces_ref[1, rows, :]
        beyond = pltpu.roll(right, before_edge, 1)
        if count > 1:
            tiles[1] = jnp.where(lane == LANES - 1, pltpu.roll(right, at_edge, 1), tiles[1])
        whole = jnp.concatenate(tiles, axis=1)
        lower.append(whole)
        above = pltpu.roll(whole, NC - 1, 1)
        last = jnp.where(lane == LANES - 1, beyond, above[:, LANES:])
        upper.append(jnp.concatenate([above[:, :LANES], last], axis=1))
    return lower, upper


def predict(count, load, faces_at, sink, half_ref, prev_ref):
    def step(i, carry):
        cons = load(i)
        prim = primitive(cons)
        speed = sound(prim)
        flux = flux_of(prim, cons, 1)
        reach = jnp.abs(prim[1]) + speed

        @pl.when(i > 0)
        def _():
            low_reach = prev_ref[1, pl.ds(0, NZ), :]
            rad = twice_face(row_of(prev_ref, 0), load(i - 1), low_reach, flux, cons, reach)

            @pl.when(i > 1)
            def _():
                sink(i - 1, primitive([x - PRED * y for x, y in zip(row_of(half_ref, 0), rad)]))

            @pl.when(i < count - 1)
            def _():
                lower, upper = patched(first_order_faces(prim, cons, speed, 2, 1), *faces_at(i), 1)
                vert = first_order_faces(prim, cons, speed, 3, 0)
                source = added_sources(cons, prim)
                for c in range(5):
                    total = (upper[c] - lower[c]) + (pltpu.roll(vert[c], NZ - 1, 0) - vert[c]) - rad[c]
                    value = cons[c] - PRED * total
                    if c in source:
                        value = value + 0.5 * step_ratio * source[c]
                    half_ref[0, pl.ds(c * NZ, NZ), :] = value

        put_row(prev_ref, 0, flux)
        prev_ref[1, pl.ds(0, NZ), :] = reach
        return carry

    lax.fori_loop(0, count, step, 0)


def correct(count, load, cons_at, faces_ref, group_of, sink, half_ref, prev_ref):
    def step(i, carry):
        prim = load(i)
        half_slope = [0.5 * minmod(x - a, b - x) for x, a, b in zip(prim, load(i - 1), load(i + 1))]
        high = [x - s for x, s in zip(prim, half_slope)]

        @pl.when(i > 0)
        def _():
            rad = twice_face(*state_at(row_of(prev_ref, 0), 1), *state_at(high, 1))

            @pl.when(i > 1)
            def _():
                sink(i - 1, [x - CORR * y for x, y in zip(row_of(half_ref, 0), rad)])

            @pl.when(i < count - 1)
            def _():
                lower, upper = patched(second_order_faces(prim, 2, 1), faces_ref, group_of(i), 2)
                vert = second_order_faces(prim, 3, 0)
                source = added_sources(conserved_of(prim), prim)
                cons = cons_at(i)
                for c in range(5):
                    total = (upper[c] - lower[c]) + (pltpu.roll(vert[c], NZ - 1, 0) - vert[c]) - rad[c]
                    value = cons[c] - CORR * total
                    if c in source:
                        value = value + step_ratio * source[c]
                    half_ref[0, pl.ds(c * NZ, NZ), :] = value

        put_row(prev_ref, 0, [x + s for x, s in zip(prim, half_slope)])
        return carry

    lax.fori_loop(0, count, step, 0)


def prep_kernel(x_ref, xt_ref, own_ref):
    for c in range(5):
        xt_ref[:, pl.ds(c * NZ, NZ), :] = jnp.swapaxes(x_ref[pl.ds(c * NZ, NZ)], 0, 1)
    group = lanes_of((5 * NZ, LANES)) // GROUP
    packed = jnp.zeros((5 * NZ, LANES), jnp.float32)
    for row in range(NROW):
        moved = pltpu.roll(xt_ref[row], row * GROUP + GROUP // 2, 1)[:, :LANES]
        packed = jnp.where(group == row, moved, packed)
    own_ref[...] = packed


def rims_kernel(rem_ref, xt_ref, own_ref, left_ref, right_ref, strip_ref, up_ref, dn_ref, end_ref):
    lane = lanes_of((5 * NZ, LANES))
    from_low = (lane % GROUP) < GROUP // 2
    own = own_ref[...]
    low = jnp.where(from_low, left_ref[...], own)
    high = jnp.where(from_low, own, right_ref[...])
    strip_ref[:, :LANES] = low
    strip_ref[:, LANES:] = high
    for ref, first in ((dn_ref, 0), (up_ref, NROW - WIDTH)):
        for w in range(WIDTH):
            for side in range(2):
                ref[2 * w + side] = xt_ref[first + w, :, side * LANES : (side + 1) * LANES]
        three = WIDTH * GROUP
        by = (-first * GROUP) % LANES
        a, b = low, pltpu.roll(high, (by + three) % LANES, 1)
        if by:
            a = pltpu.roll(low, by, 1)
        ref[2 * WIDTH] = jnp.where(lane < three, a, b)

    at_low = rem_ref[1] == 0
    first = jnp.where(at_low, 0, NROW - WIDTH)
    by = jnp.where(at_low, NC - rem_ref[0], rem_ref[0])
    strips = jnp.zeros((5 * NZ, LANES), jnp.float32)
    for w in range(WIDTH):
        row = first + w
        main = xt_ref[row]
        moved = pltpu.roll(main, jnp.bitwise_and(by, NC - 1), 1)
        end_ref[2 * w] = moved[:, :LANES]
        end_ref[2 * w + 1] = moved[:, LANES:]
        above = pltpu.roll(high, jnp.bitwise_and(2 * LANES - GROUP * row - GROUP // 2, LANES - 1), 1)
        below = pltpu.roll(low, jnp.bitwise_and(2 * LANES - GROUP * row - GROUP // 2, LANES - 1), 1)
        wide = jnp.concatenate([main, above, below], axis=1)
        cut = pltpu.roll(wide, jnp.bitwise_and(by - (NC - GROUP // 2) + w * GROUP + 2 * NC, 2 * NC - 1), 1)
        strips = jnp.where(lane // GROUP == w, cut[:, :LANES], strips)
    end_ref[2 * WIDTH] = strips


def inner_kernel(xt_ref, strip_ref, out_ref, kept_ref, prim_ref, half_ref, prev_ref, first_ref, second_ref):
    cons = row_of(strip_ref)
    prim, speed, az = edge_faces_of(cons)
    keep_faces(first_ref, az)
    half = strip_half(cons, prim, speed, az, rolled(cons, GROUP, 1), rolled(cons, -GROUP, 1))
    keep_faces(second_ref, second_order_faces(primitive(half), 2, 1))
    predict(
        NROW,
        lambda i: row_of(xt_ref, i),
        lambda i: (first_ref, i),
        lambda i, arrays: put_row(prim_ref, i, arrays),
        half_ref,
        prev_ref,
    )
    for n in range(4):
        kept_ref[n] = prim_ref[1 + n]
        kept_ref[4 + n] = prim_ref[NROW - 5 + n]
    correct(
        NROW - 4,
        lambda i: row_of(prim_ref, i + 2),
        lambda i: row_of(xt_ref, i + 2),
        second_ref,
        lambda i: i + 2,
        lambda i, arrays: put_row(out_ref, i + 2, arrays),
        half_ref,
        prev_ref,
    )


def outer_kernel(
    rem_ref, xt_ref, strip_ref, kept_ref, up_ref, dn_ref, e1_ref, e2_ref, in_ref, out_ref,
    cons_ref, prim_ref, half_ref, prev_ref, first_ref, second_ref, ghost_ref, strips_ref,
):
    out_ref[pl.ds(WIDTH, NROW - 2 * WIDTH)] = in_ref[pl.ds(WIDTH, NROW - 2 * WIDTH)]
    rem, rad, last = rem_ref[0], rem_ref[1], rem_ref[2]
    lane = lanes_of((5 * NZ, LANES))
    three = WIDTH * GROUP

    def own_side(seg, ref):
        for w in range(WIDTH):
            for side in range(2):
                cons_ref[seg, WIDTH * seg + w, :, side * LANES : (side + 1) * LANES] = ref[2 * w + side]

    def end_side(seg, upper_ref, lower_ref, cut):
        for w in range(WIDTH):
            for side in range(2):
                cons_ref[seg, WIDTH * seg + w, :, side * LANES : (side + 1) * LANES] = jnp.where(
                    lane + side * LANES >= cut, upper_ref[2 * w + side], lower_ref[2 * w + side]
                )

    @pl.when(rad != 0)
    def _():
        own_side(0, up_ref)
        strips_ref[0] = up_ref[2 * WIDTH]
        strips_ref[1] = pltpu.roll(up_ref[2 * WIDTH], LANES - three, 1)

    @pl.when(rad == 0)
    def _():
        end_side(0, e1_ref, e2_ref, rem)
        strips_ref[0] = e2_ref[2 * WIDTH]
        strips_ref[1] = e1_ref[2 * WIDTH]

    @pl.when(rad != last)
    def _():
        own_side(1, dn_ref)
        strips_ref[0] = jnp.where(lane < three, strips_ref[0], pltpu.roll(dn_ref[2 * WIDTH], three, 1))
        strips_ref[1] = jnp.where(lane < three, strips_ref[1], dn_ref[2 * WIDTH])

    @pl.when(rad == last)
    def _():
        end_side(1, e2_ref, e1_ref, NC - rem)
        strips_ref[0] = jnp.where(lane < three, strips_ref[0], pltpu.roll(e1_ref[2 * WIDTH], three, 1))
        strips_ref[1] = jnp.where(lane < three, strips_ref[1], pltpu.roll(e2_ref[2 * WIDTH], three, 1))

    for w in range(WIDTH):
        cons_ref[0, WIDTH + w] = xt_ref[w]
        cons_ref[1, w] = xt_ref[NROW - WIDTH + w]
    for n in range(4):
        prim_ref[0, 3 + n] = kept_ref[n]
        prim_ref[1, n] = kept_ref[4 + n]

    ghost = [
        jnp.concatenate([strips_ref[0, pl.ds(c * NZ, NZ), :], strips_ref[1, pl.ds(c * NZ, NZ), :]], axis=1)
        for c in range(5)
    ]
    keep_faces(ghost_ref, edge_faces_of(ghost)[2])
    cons = row_of(strip_ref)
    prim, speed, az = edge_faces_of(cons)
    keep_faces(first_ref, az)
    in_tile = lanes_of((NZ, NC)) % LANES
    below = [
        jnp.where(in_tile < GROUP, a, b) for a, b in zip(rolled(ghost, -2 * GROUP, 1), rolled(cons, GROUP, 1))
    ]
    above = [
        jnp.where(in_tile >= LANES - GROUP, a, b)
        for a, b in zip(rolled(ghost, LANES - 4 * GROUP, 1), rolled(cons, -GROUP, 1))
    ]
    half = strip_half(cons, prim, speed, az, below, above)
    keep_faces(second_ref, second_order_faces(primitive(half), 2, 1))

    group = lanes_of((NZ, LANES)) // GROUP
    for side in range(2):
        for c in range(5):
            rows = pl.ds(c * NZ, NZ)
            mine = first_ref[side, rows, :]
            both = ghost_ref[side, rows, :]
            seg0 = jnp.where(group == 3, pltpu.roll(mine, 3 * GROUP, 1), both)
            seg1 = jnp.where(group == 1, pltpu.roll(mine, 2 * GROUP, 1), pltpu.roll(both, LANES - GROUP, 1))
            ghost_ref[side, rows, :] = seg0
            first_ref[side, rows, :] = seg1

    for seg in range(2):
        predict(
            5,
            lambda i: row_of(cons_ref, seg, i + seg),
            lambda i: ((ghost_ref, first_ref)[seg], i),
            lambda i, arrays: put_row(prim_ref.at[seg], i - 1 + 4 * seg, arrays),
            half_ref,
            prev_ref,
        )
        correct(
            5,
            lambda i: row_of(prim_ref, seg, i + 1),
            lambda i: row_of(cons_ref, seg, i + 2 - 3 * seg),
            second_ref,
            lambda i: i - 1 if seg == 0 else i + NROW - 4,
            lambda i, arrays: put_row(out_ref, i - 1 if seg == 0 else i + NROW - 4, arrays),
            half_ref,
            prev_ref,
        )


def remap_kernel(count, shift_ref, frac_ref, x_ref, o_ref, held_ref):
    row = shift_ref[NROW]
    shift, frac = shift_ref[row], frac_ref[row]
    hop = jnp.bitwise_and(jnp.right_shift(shift, 8), count - 1)
    rem = jnp.bitwise_and(shift, NC - 1)
    lane = lanes_of((5 * NZ, NC))

    def one(m, carry):
        here = jnp.bitwise_and(m + count - 1, count - 1)
        before = jnp.bitwise_and(m + count - 2, count - 1)
        block = x_ref[here]
        lower = jnp.where(lane == 0, pltpu.roll(x_ref[before], 1, 1), pltpu.roll(block, 1, 1))
        moved = pltpu.roll((1.0 - frac) * block + frac * lower, rem, 1)

        @pl.when(m > 0)
        def _():
            o_ref[jnp.bitwise_and(m + hop + count - 1, count - 1)] = jnp.where(lane >= rem, moved, held_ref[...])

        held_ref[...] = moved
        return carry

    lax.fori_loop(0, count + 1, one, 0)


def finish_kernel(y_ref, o_ref):
    for c in range(5):
        o_ref[pl.ds(c * NZ, NZ)] = jnp.swapaxes(y_ref[:, pl.ds(c * NZ, NZ), :], 0, 1)


def shape(*dims):
    return jax.ShapeDtypeStruct(dims, jnp.float32)


def local(conserved, shift_cells, shift_frac, boundary_offset):
    azs, rads = lax.axis_size("az"), lax.axis_size("rad")
    az, rad = lax.axis_index("az"), lax.axis_index("rad")
    offset = boundary_offset[0]
    hop, rem = offset // NC, offset % NC
    scalars = jnp.stack([rem, rad, jnp.int32(rads - 1)]).astype(jnp.int32)
    row_shape, strip_shape = (5 * NZ, NC), (5 * NZ, LANES)
    rows, own = pl.pallas_call(
        prep_kernel,
        out_shape=(shape(NROW, *row_shape), shape(*strip_shape)),
        in_specs=[VMEM],
        out_specs=(VMEM,) * 2,
        compiler_params=PARAMS,
    )(conserved.reshape(5 * NZ, NROW, NC))
    left = lax.ppermute(own, "az", [(i, (i + 1) % azs) for i in range(azs)])
    right = lax.ppermute(own, "az", [((i + 1) % azs, i) for i in range(azs)])
    rim = shape(2 * WIDTH + 1, *strip_shape)
    strip, up, dn, end = pl.pallas_call(
        rims_kernel,
        out_shape=(shape(*row_shape), rim, rim, rim),
        in_specs=[SMEM] + [VMEM] * 4,
        out_specs=(VMEM,) * 4,
        compiler_params=PARAMS,
    )(scalars, rows, own, left, right)
    from_below = lax.ppermute(up, "rad", [(i, i + 1) for i in range(rads - 1)])
    from_above = lax.ppermute(dn, "rad", [(i + 1, i) for i in range(rads - 1)])

    scratch = [
        pltpu.VMEM((1, *row_shape), jnp.float32),
        pltpu.VMEM((2, *row_shape), jnp.float32),
        pltpu.VMEM((2, *strip_shape), jnp.float32),
        pltpu.VMEM((2, *strip_shape), jnp.float32),
    ]

    def inner(rows, strip):
        return pl.pallas_call(
            inner_kernel,
            out_shape=(shape(NROW, *row_shape), shape(8, *row_shape)),
            in_specs=[VMEM] * 2,
            out_specs=(VMEM,) * 2,
            scratch_shapes=[pltpu.VMEM((NROW, *row_shape), jnp.float32), *scratch],
            compiler_params=PARAMS,
            cost_estimate=pl.CostEstimate(flops=30 * 10**6, bytes_accessed=4 * 2**20, transcendentals=0),
        )(rows, strip)

    def ends(k):
        pairs = [(a * rads + rads - 1, (a + k) % azs * rads) for a in range(azs)]
        return pairs + [(b, a) for a, b in pairs]

    def moved_by(k):
        def send(block, rows, strip):
            first, second = (lax.ppermute(block, ("az", "rad"), ends(j % azs)) for j in (k, k + 1))
            return first, second, *inner(rows, strip)

        return send

    first, second, updated, kept = lax.switch(hop, [moved_by(k) for k in range(azs)], end, rows, strip)
    updated = pl.pallas_call(
        outer_kernel,
        out_shape=shape(NROW, *row_shape),
        in_specs=[SMEM] + [VMEM] * 8,
        out_specs=VMEM,
        scratch_shapes=[
            pltpu.VMEM((2, 6, *row_shape), jnp.float32),
            pltpu.VMEM((2, 7, *row_shape), jnp.float32),
            *scratch,
            pltpu.VMEM((2, *strip_shape), jnp.float32),
            pltpu.VMEM((2, *strip_shape), jnp.float32),
        ],
        compiler_params=PARAMS,
    )(scalars, rows, strip, kept, from_below, from_above, first, second, updated)

    whole_row = lax.all_to_all(updated, "az", 0, 0, tiled=True)
    shifts = jnp.concatenate([shift_cells, az[None].astype(jnp.int32)])
    moved = pl.pallas_call(
        functools.partial(remap_kernel, azs),
        out_shape=shape(azs, *row_shape),
        in_specs=[SMEM, SMEM, VMEM],
        out_specs=VMEM,
        scratch_shapes=[pltpu.VMEM(row_shape, jnp.float32)],
        compiler_params=PARAMS,
    )(shifts, shift_frac, whole_row)
    back = lax.all_to_all(moved, "az", 0, 0, tiled=True)
    result = pl.pallas_call(
        finish_kernel,
        out_shape=shape(5 * NZ, NROW, NC),
        in_specs=[VMEM],
        out_specs=VMEM,
        compiler_params=PARAMS,
    )(back)
    return result.reshape(5, NZ, NROW, NC)


def solution(mesh):
    in_specs = (P(None, None, "rad", "az"), P("rad"), P("rad"), P())
    out_specs = P(None, None, "rad", "az")
    return jax.shard_map(local, mesh=mesh, in_specs=in_specs, out_specs=out_specs, check_vma=False)
```

```python
import functools

import jax
import jax.numpy as jnp
from jax import lax
from jax.experimental import pallas as pl
from jax.experimental.pallas import tpu as pltpu
from jax.sharding import PartitionSpec as P

gamma_ratio = 5.0 / 3.0
step_ratio = 0.06
omega_rate = 1.0
shear_rate = 1.5

NZ = 16
NROW = 16
NC = 256
LANES = 128
WIDTH = 3
PRED = 0.25 * step_ratio
CORR = 0.5 * step_ratio
GROUP = 8
VMEM = pl.BlockSpec(memory_space=pltpu.VMEM)
ANY = pl.BlockSpec(memory_space=pl.ANY)
SMEM = pl.BlockSpec(memory_space=pltpu.SMEM)
PARAMS = pltpu.CompilerParams(vmem_limit_bytes=48 * 2**20)


def lanes_of(shape):
    return lax.broadcasted_iota(jnp.int32, shape, len(shape) - 1)


def reciprocal(x):
    guess = pl.reciprocal(x, approx=True)
    return guess * (2.0 - x * guess)


def primitive(cons):
    inverse = reciprocal(cons[0])
    vel = [cons[n] * inverse for n in (1, 2, 3)]
    kinetic = 0.5 * (cons[1] * vel[0] + cons[2] * vel[1] + cons[3] * vel[2])
    return [cons[0], *vel, (gamma_ratio - 1.0) * (cons[4] - kinetic)]


def conserved_of(prim):
    mom = [prim[0] * prim[n] for n in (1, 2, 3)]
    kinetic = 0.5 * (mom[0] * prim[1] + mom[1] * prim[2] + mom[2] * prim[3])
    return [prim[0], *mom, prim[4] * (1.0 / (gamma_ratio - 1.0)) + kinetic]


def sound(prim):
    scaled = gamma_ratio * prim[4]
    return scaled * lax.rsqrt(scaled * prim[0])


def flux_of(prim, cons, normal):
    speed = prim[normal]
    flux = [cons[normal]]
    for n in (1, 2, 3):
        term = cons[n] * speed
        flux.append(term + prim[4] if n == normal else term)
    flux.append((cons[4] + prim[4]) * speed)
    return flux


def twice_face(low_flux, low_cons, low_reach, flux, cons, reach):
    top = jnp.maximum(low_reach, reach)
    return [(a + b) - top * (v - u) for a, b, u, v in zip(low_flux, flux, low_cons, cons)]


def minmod(a, b):
    return jnp.maximum(jnp.minimum(a, b), 0.0) + jnp.minimum(jnp.maximum(a, b), 0.0)


def rolled(arrays, by, axis):
    return [pltpu.roll(x, by % x.shape[axis], axis) for x in arrays]


def first_order_faces(prim, cons, speed_of_sound, normal, axis):
    flux = flux_of(prim, cons, normal)
    reach = jnp.abs(prim[normal]) + speed_of_sound
    low_cons = rolled(cons, 1, axis)
    low_flux = [low_cons[normal], *rolled(flux[1:], 1, axis)]
    low_reach = pltpu.roll(reach, 1, axis)
    return twice_face(low_flux, low_cons, low_reach, flux, cons, reach)


def state_at(prim, normal):
    cons = conserved_of(prim)
    return flux_of(prim, cons, normal), cons, jnp.abs(prim[normal]) + sound(prim)


def second_order_faces(prim, normal, axis):
    diff = [x - y for x, y in zip(prim, rolled(prim, 1, axis))]
    half_slope = [0.5 * minmod(a, b) for a, b in zip(diff, rolled(diff, -1, axis))]
    low = rolled([x + s for x, s in zip(prim, half_slope)], 1, axis)
    high = [x - s for x, s in zip(prim, half_slope)]
    return twice_face(*state_at(low, normal), *state_at(high, normal))


def added_sources(cons, prim):
    return {
        1: 2.0 * omega_rate * cons[2],
        2: -(2.0 - shear_rate) * omega_rate * cons[1],
        4: shear_rate * omega_rate * cons[1] * prim[2],
    }


def row_of(ref, *index):
    return [ref[(*index, pl.ds(c * NZ, NZ), slice(None))] for c in range(5)]


def put_row(ref, index, arrays):
    for c in range(5):
        ref[index, pl.ds(c * NZ, NZ), :] = arrays[c]


def tile_lanes():
    return lanes_of((NZ, LANES))


def edge_faces_of(strip):
    prim = primitive(strip)
    speed = sound(prim)
    return prim, speed, first_order_faces(prim, strip, speed, 2, 1)


def keep_faces(ref, faces):
    for c in range(5):
        for side in range(2):
            ref[side, pl.ds(c * NZ, NZ), :] = faces[c][:, side * LANES : (side + 1) * LANES]


def strip_half(cons, prim, speed, az, below, above):
    def rad_state(u):
        q = primitive(u)
        return flux_of(q, u, 1), u, jnp.abs(q[1]) + sound(q)

    mid_state = (flux_of(prim, cons, 1), cons, jnp.abs(prim[1]) + speed)
    rad_low = twice_face(*rad_state(below), *mid_state)
    rad_high = twice_face(*mid_state, *rad_state(above))
    vert = first_order_faces(prim, cons, speed, 3, 0)
    source = added_sources(cons, prim)
    half = []
    for c in range(5):
        total = (rad_high[c] - rad_low[c]) + (pltpu.roll(az[c], NC - 1, 1) - az[c])
        total = total + (pltpu.roll(vert[c], NZ - 1, 0) - vert[c])
        value = cons[c] - PRED * total
        half.append(value + 0.5 * step_ratio * source[c] if c in source else value)
    return half


def patched(faces, faces_ref, group, count):
    lane = tile_lanes()
    lower, upper = [], []
    for c in range(5):
        rows = pl.ds(c * NZ, NZ)
        at_edge = (2 * LANES - GROUP * group - GROUP // 2) % LANES
        before_edge = (3 * LANES - 1 - GROUP * group - GROUP // 2) % LANES
        left = pltpu.roll(faces_ref[0, rows, :], at_edge, 1)
        tiles = [jnp.where(lane < count, left, faces[c][:, :LANES]), faces[c][:, LANES:]]
        right = faces_ref[1, rows, :]
        beyond = pltpu.roll(right, before_edge, 1)
        if count > 1:
            tiles[1] = jnp.where(lane == LANES - 1, pltpu.roll(right, at_edge, 1), tiles[1])
        whole = jnp.concatenate(tiles, axis=1)
        lower.append(whole)
        above = pltpu.roll(whole, NC - 1, 1)
        last = jnp.where(lane == LANES - 1, beyond, above[:, LANES:])
        upper.append(jnp.concatenate([above[:, :LANES], last], axis=1))
    return lower, upper


def predict(count, load, faces_at, sink, save_ref, unroll):
    def state(i):
        cons = load(i)
        prim = primitive(cons)
        speed = sound(prim)
        return cons, prim, speed, (flux_of(prim, cons, 1), cons, jnp.abs(prim[1]) + speed)

    def keep(prim, speed, rad_state, rad):
        put_row(save_ref, 0, rad_state[0])
        put_row(save_ref, 1, rad)
        put_row(save_ref, 2, prim)
        save_ref[3, pl.ds(0, NZ), :] = speed
        save_ref[3, pl.ds(NZ, NZ), :] = rad_state[2]

    _, _, _, before = state(0)
    _, prim, speed, here = state(1)
    keep(prim, speed, here, twice_face(*before, *here))

    def step(i, carry):
        cons = load(i)
        low = row_of(save_ref, 1)
        prim = row_of(save_ref, 2)
        speed = save_ref[3, pl.ds(0, NZ), :]
        here = (row_of(save_ref, 0), cons, save_ref[3, pl.ds(NZ, NZ), :])
        _, next_prim, next_speed, there = state(i + 1)
        rad = twice_face(*here, *there)
        keep(next_prim, next_speed, there, rad)
        total = [x - y for x, y in zip(rad, low)]
        vert = first_order_faces(prim, cons, speed, 3, 0)
        total = [t + (pltpu.roll(x, NZ - 1, 0) - x) for t, x in zip(total, vert)]
        lower, upper = patched(first_order_faces(prim, cons, speed, 2, 1), *faces_at(i), 1)
        source = added_sources(cons, prim)
        half = []
        for c in range(5):
            value = cons[c] - PRED * (total[c] + (upper[c] - lower[c]))
            half.append(value + 0.5 * step_ratio * source[c] if c in source else value)
        sink(i, primitive(half))
        return carry

    lax.fori_loop(1, count - 1, step, 0, unroll=unroll)


def correct(count, load, cons_at, faces_ref, group_of, sink, save_ref, unroll):
    def sides(i):
        prim = load(i)
        half_slope = [0.5 * minmod(x - a, b - x) for x, a, b in zip(prim, load(i - 1), load(i + 1))]
        return [x - s for x, s in zip(prim, half_slope)], [x + s for x, s in zip(prim, half_slope)]

    _, above = sides(0)
    high, upper_side = sides(1)
    put_row(save_ref, 0, upper_side)
    put_row(save_ref, 1, twice_face(*state_at(above, 1), *state_at(high, 1)))

    def step(i, carry):
        below = row_of(save_ref, 0)
        low = row_of(save_ref, 1)
        high, upper_side = sides(i + 1)
        rad = twice_face(*state_at(below, 1), *state_at(high, 1))
        put_row(save_ref, 0, upper_side)
        put_row(save_ref, 1, rad)
        total = [x - y for x, y in zip(rad, low)]
        prim = load(i)
        vert = second_order_faces(prim, 3, 0)
        total = [t + (pltpu.roll(x, NZ - 1, 0) - x) for t, x in zip(total, vert)]
        lower, upper = patched(second_order_faces(prim, 2, 1), faces_ref, group_of(i), 2)
        source = added_sources(conserved_of(prim), prim)
        cons = cons_at(i)
        done = []
        for c in range(5):
            value = cons[c] - CORR * (total[c] + (upper[c] - lower[c]))
            done.append(value + step_ratio * source[c] if c in source else value)
        sink(i, done)
        return carry

    lax.fori_loop(1, count - 1, step, 0, unroll=unroll)


def loop_scratch():
    return [
        pltpu.VMEM((4, 5 * NZ, NC), jnp.float32),
        pltpu.VMEM((2, 5 * NZ, LANES), jnp.float32),
        pltpu.VMEM((2, 5 * NZ, LANES), jnp.float32),
    ]


def prep_kernel(x_ref, xt_ref, own_ref):
    for c in range(5):
        xt_ref[:, pl.ds(c * NZ, NZ), :] = jnp.swapaxes(x_ref[pl.ds(c * NZ, NZ)], 0, 1)
    group = lanes_of((5 * NZ, LANES)) // GROUP
    packed = jnp.zeros((5 * NZ, LANES), jnp.float32)
    for row in range(NROW):
        moved = pltpu.roll(xt_ref[row], row * GROUP + GROUP // 2, 1)[:, :LANES]
        packed = jnp.where(group == row, moved, packed)
    own_ref[...] = packed


def rims_kernel(rem_ref, xt_ref, own_ref, left_ref, right_ref, strip_ref, up_ref, dn_ref, end_ref):
    lane = lanes_of((5 * NZ, LANES))
    from_low = (lane % GROUP) < GROUP // 2
    own = own_ref[...]
    low = jnp.where(from_low, left_ref[...], own)
    high = jnp.where(from_low, own, right_ref[...])
    strip_ref[:, :LANES] = low
    strip_ref[:, LANES:] = high
    for ref, first in ((dn_ref, 0), (up_ref, NROW - WIDTH)):
        for w in range(WIDTH):
            for side in range(2):
                ref[2 * w + side] = xt_ref[first + w, :, side * LANES : (side + 1) * LANES]
        three = WIDTH * GROUP
        by = (-first * GROUP) % LANES
        a, b = low, pltpu.roll(high, (by + three) % LANES, 1)
        if by:
            a = pltpu.roll(low, by, 1)
        ref[2 * WIDTH] = jnp.where(lane < three, a, b)

    at_low = rem_ref[1] == 0
    first = jnp.where(at_low, 0, NROW - WIDTH)
    by = jnp.where(at_low, NC - rem_ref[0], rem_ref[0])
    strips = jnp.zeros((5 * NZ, LANES), jnp.float32)
    for w in range(WIDTH):
        row = first + w
        main = xt_ref[row]
        moved = pltpu.roll(main, jnp.bitwise_and(by, NC - 1), 1)
        end_ref[2 * w] = moved[:, :LANES]
        end_ref[2 * w + 1] = moved[:, LANES:]
        above = pltpu.roll(high, jnp.bitwise_and(2 * LANES - GROUP * row - GROUP // 2, LANES - 1), 1)
        below = pltpu.roll(low, jnp.bitwise_and(2 * LANES - GROUP * row - GROUP // 2, LANES - 1), 1)
        wide = jnp.concatenate([main, above, below], axis=1)
        cut = pltpu.roll(wide, jnp.bitwise_and(by - (NC - GROUP // 2) + w * GROUP + 2 * NC, 2 * NC - 1), 1)
        strips = jnp.where(lane // GROUP == w, cut[:, :LANES], strips)
    end_ref[2 * WIDTH] = strips


def inner_kernel(xt_ref, strip_ref, out_ref, kept_ref, prim_ref, save_ref, first_ref, second_ref):
    cons = row_of(strip_ref)
    prim, speed, az = edge_faces_of(cons)
    keep_faces(first_ref, az)
    half = strip_half(cons, prim, speed, az, rolled(cons, GROUP, 1), rolled(cons, -GROUP, 1))
    keep_faces(second_ref, second_order_faces(primitive(half), 2, 1))
    predict(
        NROW,
        lambda i: row_of(xt_ref, i),
        lambda i: (first_ref, i),
        lambda i, arrays: put_row(prim_ref, i, arrays),
        save_ref,
        2,
    )
    for n in range(4):
        kept_ref[n] = prim_ref[1 + n]
        kept_ref[4 + n] = prim_ref[NROW - 5 + n]
    correct(
        NROW - 4,
        lambda i: row_of(prim_ref, i + 2),
        lambda i: row_of(xt_ref, i + 2),
        second_ref,
        lambda i: i + 2,
        lambda i, arrays: put_row(out_ref, i + 2, arrays),
        save_ref,
        2,
    )


def outer_kernel(
    rem_ref, xt_ref, strip_ref, kept_ref, up_ref, dn_ref, e1_ref, e2_ref, seen_ref, in_ref, whole_ref,
    cons_ref, prim_ref, save_ref, first_ref, second_ref, ghost_ref, strips_ref,
    out_ref, sem,
):
    del seen_ref, in_ref
    rem, rad, last = rem_ref[0], rem_ref[1], rem_ref[2]
    lane = lanes_of((5 * NZ, LANES))
    three = WIDTH * GROUP

    def own_side(seg, ref):
        for w in range(WIDTH):
            for side in range(2):
                cons_ref[seg, WIDTH * seg + w, :, side * LANES : (side + 1) * LANES] = ref[2 * w + side]

    def end_side(seg, upper_ref, lower_ref, cut):
        for w in range(WIDTH):
            for side in range(2):
                cons_ref[seg, WIDTH * seg + w, :, side * LANES : (side + 1) * LANES] = jnp.where(
                    lane + side * LANES >= cut, upper_ref[2 * w + side], lower_ref[2 * w + side]
                )

    @pl.when(rad != 0)
    def _():
        own_side(0, up_ref)
        strips_ref[0] = up_ref[2 * WIDTH]
        strips_ref[1] = pltpu.roll(up_ref[2 * WIDTH], LANES - three, 1)

    @pl.when(rad == 0)
    def _():
        end_side(0, e1_ref, e2_ref, rem)
        strips_ref[0] = e2_ref[2 * WIDTH]
        strips_ref[1] = e1_ref[2 * WIDTH]

    @pl.when(rad != last)
    def _():
        own_side(1, dn_ref)
        strips_ref[0] = jnp.where(lane < three, strips_ref[0], pltpu.roll(dn_ref[2 * WIDTH], three, 1))
        strips_ref[1] = jnp.where(lane < three, strips_ref[1], dn_ref[2 * WIDTH])

    @pl.when(rad == last)
    def _():
        end_side(1, e2_ref, e1_ref, NC - rem)
        strips_ref[0] = jnp.where(lane < three, strips_ref[0], pltpu.roll(e1_ref[2 * WIDTH], three, 1))
        strips_ref[1] = jnp.where(lane < three, strips_ref[1], pltpu.roll(e2_ref[2 * WIDTH], three, 1))

    for w in range(WIDTH):
        cons_ref[0, WIDTH + w] = xt_ref[w]
        cons_ref[1, w] = xt_ref[NROW - WIDTH + w]
    for n in range(4):
        prim_ref[0, 3 + n] = kept_ref[n]
        prim_ref[1, n] = kept_ref[4 + n]

    ghost = [
        jnp.concatenate([strips_ref[0, pl.ds(c * NZ, NZ), :], strips_ref[1, pl.ds(c * NZ, NZ), :]], axis=1)
        for c in range(5)
    ]
    keep_faces(ghost_ref.at[0], edge_faces_of(ghost)[2])
    cons = row_of(strip_ref)
    prim, speed, az = edge_faces_of(cons)
    keep_faces(first_ref, az)
    in_tile = lanes_of((NZ, NC)) % LANES
    below = [
        jnp.where(in_tile < GROUP, a, b) for a, b in zip(rolled(ghost, -2 * GROUP, 1), rolled(cons, GROUP, 1))
    ]
    above = [
        jnp.where(in_tile >= LANES - GROUP, a, b)
        for a, b in zip(rolled(ghost, LANES - 4 * GROUP, 1), rolled(cons, -GROUP, 1))
    ]
    half = strip_half(cons, prim, speed, az, below, above)
    keep_faces(second_ref, second_order_faces(primitive(half), 2, 1))

    group = lanes_of((5 * NZ, LANES)) // GROUP
    for side in range(2):
        mine, both = first_ref[side], ghost_ref[0, side]
        ghost_ref[0, side] = jnp.where(group == 3, pltpu.roll(mine, 3 * GROUP, 1), both)
        ghost_ref[1, side] = jnp.where(group == 1, pltpu.roll(mine, 2 * GROUP, 1), pltpu.roll(both, LANES - GROUP, 1))

    def segment(seg, carry):
        predict(
            5,
            lambda i: row_of(cons_ref, seg, i + seg),
            lambda i: (ghost_ref.at[seg], i),
            lambda i, arrays: put_row(prim_ref.at[seg], i - 1 + 4 * seg, arrays),
            save_ref,
            1,
        )
        correct(
            5,
            lambda i: row_of(prim_ref, seg, i + 1),
            lambda i: row_of(cons_ref, seg, i + 2 - 3 * seg),
            second_ref,
            lambda i: i - 1 + 13 * seg,
            lambda i, arrays: put_row(out_ref.at[seg], i - 1, arrays),
            save_ref,
            1,
        )
        return carry

    lax.fori_loop(0, 2, segment, 0)
    copies = [
        pltpu.make_async_copy(out_ref.at[seg], whole_ref.at[pl.ds(seg * (NROW - WIDTH), WIDTH)], sem.at[seg])
        for seg in range(2)
    ]
    for copy in copies:
        copy.start()
    for copy in copies:
        copy.wait()


def remap_kernel(count, shift_ref, frac_ref, x_ref, o_ref):
    row = shift_ref[NROW]
    shift, frac = shift_ref[row], frac_ref[row]
    tiles = 2 * count
    hop = jnp.bitwise_and(jnp.right_shift(shift, 7), tiles - 1)
    rem = jnp.bitwise_and(shift, LANES - 1)
    lane = lanes_of((5 * NZ, LANES))
    near, far = lane >= rem, lane > rem
    rest = 1.0 - frac

    def place(k):
        start = pl.multiple_of(jnp.bitwise_and(k, 1) * LANES, LANES)
        return jnp.right_shift(k, 1), slice(None), pl.ds(start, LANES)

    def turned(k):
        tile = x_ref[place(k)]
        return pltpu.roll(tile, rem, 1), pltpu.roll(tile, jnp.bitwise_and(rem + 1, LANES - 1), 1)

    def one(k, before):
        here = turned(k)
        value = rest * jnp.where(near, here[0], before[0]) + frac * jnp.where(far, here[1], before[1])
        o_ref[place(jnp.bitwise_and(k + hop, tiles - 1))] = value
        return here

    lax.fori_loop(0, tiles, one, turned(jnp.int32(tiles - 1)), unroll=2)


def finish_kernel(y_ref, o_ref):
    for c in range(5):
        o_ref[pl.ds(c * NZ, NZ)] = jnp.swapaxes(y_ref[:, pl.ds(c * NZ, NZ), :], 0, 1)


def shape(*dims):
    return jax.ShapeDtypeStruct(dims, jnp.float32)


def local(conserved, shift_cells, shift_frac, boundary_offset):
    azs, rads = lax.axis_size("az"), lax.axis_size("rad")
    az, rad = lax.axis_index("az"), lax.axis_index("rad")
    offset = boundary_offset[0]
    hop, rem = offset // NC, offset % NC
    scalars = jnp.stack([rem, rad, jnp.int32(rads - 1)]).astype(jnp.int32)
    row_shape, strip_shape = (5 * NZ, NC), (5 * NZ, LANES)
    rows, own = pl.pallas_call(
        prep_kernel,
        out_shape=(shape(NROW, *row_shape), shape(*strip_shape)),
        in_specs=[VMEM],
        out_specs=(VMEM,) * 2,
        compiler_params=PARAMS,
    )(conserved.reshape(5 * NZ, NROW, NC))
    left = lax.ppermute(own, "az", [(i, (i + 1) % azs) for i in range(azs)])
    right = lax.ppermute(own, "az", [((i + 1) % azs, i) for i in range(azs)])
    rim = shape(2 * WIDTH + 1, *strip_shape)
    strip, up, dn, end = pl.pallas_call(
        rims_kernel,
        out_shape=(shape(*row_shape), rim, rim, rim),
        in_specs=[SMEM] + [VMEM] * 4,
        out_specs=(VMEM,) * 4,
        compiler_params=PARAMS,
    )(scalars, rows, own, left, right)
    scratch = loop_scratch()

    def inner(rows, strip):
        return pl.pallas_call(
            inner_kernel,
            out_shape=(shape(NROW, *row_shape), shape(8, *row_shape)),
            in_specs=[VMEM] * 2,
            out_specs=(VMEM,) * 2,
            scratch_shapes=[pltpu.VMEM((NROW, *row_shape), jnp.float32), *scratch],
            compiler_params=PARAMS,
            cost_estimate=pl.CostEstimate(flops=30 * 10**6, bytes_accessed=4 * 2**20, transcendentals=0),
        )(rows, strip)

    def ends(k):
        pairs = [(a * rads + rads - 1, (a + k) % azs * rads) for a in range(azs)]
        return pairs + [(b, a) for a, b in pairs]

    def moved_by(k):
        def send(block, up, dn, rows, strip):
            from_below = lax.ppermute(up, "rad", [(i, i + 1) for i in range(rads - 1)])
            from_above = lax.ppermute(dn, "rad", [(i + 1, i) for i in range(rads - 1)])
            first, second = (lax.ppermute(block, ("az", "rad"), ends(j % azs)) for j in (k, k + 1))
            seen = first[-1, :8] + second[-1, :8]
            return first, second, from_below, from_above, seen, *inner(rows, strip)

        return send

    first, second, from_below, from_above, seen, updated, kept = lax.switch(
        hop, [moved_by(k) for k in range(azs)], end, up, dn, rows, strip
    )
    updated = pl.pallas_call(
        outer_kernel,
        out_shape=shape(NROW, *row_shape),
        in_specs=[SMEM] + [VMEM] * 7 + [ANY] * 2,
        out_specs=ANY,
        input_output_aliases={9: 0},
        scratch_shapes=[
            pltpu.VMEM((2, 6, *row_shape), jnp.float32),
            pltpu.VMEM((2, 7, *row_shape), jnp.float32),
            *scratch,
            pltpu.VMEM((2, 2, *strip_shape), jnp.float32),
            pltpu.VMEM((2, *strip_shape), jnp.float32),
            pltpu.VMEM((2, WIDTH, *row_shape), jnp.float32),
            pltpu.SemaphoreType.DMA((2,)),
        ],
        compiler_params=PARAMS,
    )(scalars, rows, strip, kept, from_below, from_above, first, second, seen, updated)

    whole_row = lax.all_to_all(updated, "az", 0, 0, tiled=True)
    shifts = jnp.concatenate([shift_cells, az[None].astype(jnp.int32)])
    moved = pl.pallas_call(
        functools.partial(remap_kernel, azs),
        out_shape=shape(azs, *row_shape),
        in_specs=[SMEM, SMEM, VMEM],
        out_specs=VMEM,
        compiler_params=PARAMS,
    )(shifts, shift_frac, whole_row)
    back = lax.all_to_all(moved, "az", 0, 0, tiled=True)
    result = pl.pallas_call(
        finish_kernel,
        out_shape=shape(5 * NZ, NROW, NC),
        in_specs=[VMEM],
        out_specs=VMEM,
        compiler_params=PARAMS,
    )(back)
    return result.reshape(5, NZ, NROW, NC)


def solution(mesh):
    in_specs = (P(None, None, "rad", "az"), P("rad"), P("rad"), P())
    out_specs = P(None, None, "rad", "az")
    return jax.shard_map(local, mesh=mesh, in_specs=in_specs, out_specs=out_specs, check_vma=False)
```

```python
import functools

import jax
import jax.numpy as jnp
from jax import lax
from jax.experimental import pallas as pl
from jax.experimental.pallas import tpu as pltpu
from jax.sharding import PartitionSpec as P

gamma_ratio = 5.0 / 3.0
step_ratio = 0.06
omega_rate = 1.0
shear_rate = 1.5

NZ = 16
NROW = 16
NC = 256
LANES = 128
WIDTH = 3
PRED = 0.25 * step_ratio
CORR = 0.5 * step_ratio
GROUP = 8
VMEM = pl.BlockSpec(memory_space=pltpu.VMEM)
ANY = pl.BlockSpec(memory_space=pl.ANY)
SMEM = pl.BlockSpec(memory_space=pltpu.SMEM)
PARAMS = pltpu.CompilerParams(vmem_limit_bytes=48 * 2**20)


def lanes_of(shape):
    return lax.broadcasted_iota(jnp.int32, shape, len(shape) - 1)


def reciprocal(x):
    guess = pl.reciprocal(x, approx=True)
    return guess * (2.0 - x * guess)


def primitive(cons):
    inverse = reciprocal(cons[0])
    vel = [cons[n] * inverse for n in (1, 2, 3)]
    kinetic = 0.5 * (cons[1] * vel[0] + cons[2] * vel[1] + cons[3] * vel[2])
    return [cons[0], *vel, (gamma_ratio - 1.0) * (cons[4] - kinetic)]


def conserved_of(prim):
    mom = [prim[0] * prim[n] for n in (1, 2, 3)]
    kinetic = 0.5 * (mom[0] * prim[1] + mom[1] * prim[2] + mom[2] * prim[3])
    return [prim[0], *mom, prim[4] * (1.0 / (gamma_ratio - 1.0)) + kinetic]


def sound(prim):
    scaled = gamma_ratio * prim[4]
    return scaled * lax.rsqrt(scaled * prim[0])


def flux_of(prim, cons, normal):
    speed = prim[normal]
    flux = [cons[normal]]
    for n in (1, 2, 3):
        term = cons[n] * speed
        flux.append(term + prim[4] if n == normal else term)
    flux.append((cons[4] + prim[4]) * speed)
    return flux


def twice_face(low_flux, low_cons, low_reach, flux, cons, reach):
    top = jnp.maximum(low_reach, reach)
    return [(a + b) - top * (v - u) for a, b, u, v in zip(low_flux, flux, low_cons, cons)]


def minmod(a, b):
    return jnp.maximum(jnp.minimum(a, b), 0.0) + jnp.minimum(jnp.maximum(a, b), 0.0)


def rolled(arrays, by, axis):
    return [pltpu.roll(x, by % x.shape[axis], axis) for x in arrays]


def first_order_faces(prim, cons, speed_of_sound, normal, axis):
    flux = flux_of(prim, cons, normal)
    reach = jnp.abs(prim[normal]) + speed_of_sound
    low_cons = rolled(cons, 1, axis)
    low_flux = [low_cons[normal], *rolled(flux[1:], 1, axis)]
    low_reach = pltpu.roll(reach, 1, axis)
    return twice_face(low_flux, low_cons, low_reach, flux, cons, reach)


def state_at(prim, normal):
    cons = conserved_of(prim)
    return flux_of(prim, cons, normal), cons, jnp.abs(prim[normal]) + sound(prim)


def second_order_faces(prim, normal, axis):
    diff = [x - y for x, y in zip(prim, rolled(prim, 1, axis))]
    half_slope = [0.5 * minmod(a, b) for a, b in zip(diff, rolled(diff, -1, axis))]
    low = rolled([x + s for x, s in zip(prim, half_slope)], 1, axis)
    high = [x - s for x, s in zip(prim, half_slope)]
    return twice_face(*state_at(low, normal), *state_at(high, normal))


def added_sources(cons, prim):
    return {
        1: 2.0 * omega_rate * cons[2],
        2: -(2.0 - shear_rate) * omega_rate * cons[1],
        4: shear_rate * omega_rate * cons[1] * prim[2],
    }


def row_of(ref, *index):
    return [ref[(*index, pl.ds(c * NZ, NZ), slice(None))] for c in range(5)]


def put_row(ref, index, arrays):
    for c in range(5):
        ref[index, pl.ds(c * NZ, NZ), :] = arrays[c]


def tile_lanes():
    return lanes_of((NZ, LANES))


def edge_faces_of(strip):
    prim = primitive(strip)
    speed = sound(prim)
    return prim, speed, first_order_faces(prim, strip, speed, 2, 1)


def keep_faces(ref, faces):
    for c in range(5):
        for side in range(2):
            ref[side, pl.ds(c * NZ, NZ), :] = faces[c][:, side * LANES : (side + 1) * LANES]


def strip_half(cons, prim, speed, az, below, above):
    def rad_state(u):
        q = primitive(u)
        return flux_of(q, u, 1), u, jnp.abs(q[1]) + sound(q)

    mid_state = (flux_of(prim, cons, 1), cons, jnp.abs(prim[1]) + speed)
    rad_low = twice_face(*rad_state(below), *mid_state)
    rad_high = twice_face(*mid_state, *rad_state(above))
    vert = first_order_faces(prim, cons, speed, 3, 0)
    source = added_sources(cons, prim)
    half = []
    for c in range(5):
        total = (rad_high[c] - rad_low[c]) + (pltpu.roll(az[c], NC - 1, 1) - az[c])
        total = total + (pltpu.roll(vert[c], NZ - 1, 0) - vert[c])
        value = cons[c] - PRED * total
        half.append(value + 0.5 * step_ratio * source[c] if c in source else value)
    return half


def patched(faces, faces_ref, group, count):
    lane = tile_lanes()
    lower, upper = [], []
    for c in range(5):
        rows = pl.ds(c * NZ, NZ)
        at_edge = (2 * LANES - GROUP * group - GROUP // 2) % LANES
        before_edge = (3 * LANES - 1 - GROUP * group - GROUP // 2) % LANES
        left = pltpu.roll(faces_ref[0, rows, :], at_edge, 1)
        tiles = [jnp.where(lane < count, left, faces[c][:, :LANES]), faces[c][:, LANES:]]
        right = faces_ref[1, rows, :]
        beyond = pltpu.roll(right, before_edge, 1)
        if count > 1:
            tiles[1] = jnp.where(lane == LANES - 1, pltpu.roll(right, at_edge, 1), tiles[1])
        whole = jnp.concatenate(tiles, axis=1)
        lower.append(whole)
        above = pltpu.roll(whole, NC - 1, 1)
        last = jnp.where(lane == LANES - 1, beyond, above[:, LANES:])
        upper.append(jnp.concatenate([above[:, :LANES], last], axis=1))
    return lower, upper


def predict(count, load, faces_at, sink, save_ref, unroll):
    def state(i):
        cons = load(i)
        prim = primitive(cons)
        speed = sound(prim)
        return cons, prim, speed, (flux_of(prim, cons, 1), cons, jnp.abs(prim[1]) + speed)

    def keep(prim, speed, rad_state, rad):
        put_row(save_ref, 0, rad_state[0])
        put_row(save_ref, 1, rad)
        put_row(save_ref, 2, prim)
        save_ref[3, pl.ds(0, NZ), :] = speed
        save_ref[3, pl.ds(NZ, NZ), :] = rad_state[2]

    _, _, _, before = state(0)
    _, prim, speed, here = state(1)
    keep(prim, speed, here, twice_face(*before, *here))

    def step(i, carry):
        cons = load(i)
        low = row_of(save_ref, 1)
        prim = row_of(save_ref, 2)
        speed = save_ref[3, pl.ds(0, NZ), :]
        here = (row_of(save_ref, 0), cons, save_ref[3, pl.ds(NZ, NZ), :])
        _, next_prim, next_speed, there = state(i + 1)
        rad = twice_face(*here, *there)
        keep(next_prim, next_speed, there, rad)
        total = [x - y for x, y in zip(rad, low)]
        vert = first_order_faces(prim, cons, speed, 3, 0)
        total = [t + (pltpu.roll(x, NZ - 1, 0) - x) for t, x in zip(total, vert)]
        lower, upper = patched(first_order_faces(prim, cons, speed, 2, 1), *faces_at(i), 1)
        source = added_sources(cons, prim)
        half = []
        for c in range(5):
            value = cons[c] - PRED * (total[c] + (upper[c] - lower[c]))
            half.append(value + 0.5 * step_ratio * source[c] if c in source else value)
        sink(i, primitive(half))
        return carry

    lax.fori_loop(1, count - 1, step, 0, unroll=unroll)


def correct(count, load, cons_at, faces_ref, group_of, sink, save_ref, unroll):
    def sides(i):
        prim = load(i)
        half_slope = [0.5 * minmod(x - a, b - x) for x, a, b in zip(prim, load(i - 1), load(i + 1))]
        return [x - s for x, s in zip(prim, half_slope)], [x + s for x, s in zip(prim, half_slope)]

    _, above = sides(0)
    high, upper_side = sides(1)
    put_row(save_ref, 0, upper_side)
    put_row(save_ref, 1, twice_face(*state_at(above, 1), *state_at(high, 1)))

    def step(i, carry):
        below = row_of(save_ref, 0)
        low = row_of(save_ref, 1)
        high, upper_side = sides(i + 1)
        rad = twice_face(*state_at(below, 1), *state_at(high, 1))
        put_row(save_ref, 0, upper_side)
        put_row(save_ref, 1, rad)
        total = [x - y for x, y in zip(rad, low)]
        prim = load(i)
        vert = second_order_faces(prim, 3, 0)
        total = [t + (pltpu.roll(x, NZ - 1, 0) - x) for t, x in zip(total, vert)]
        lower, upper = patched(second_order_faces(prim, 2, 1), faces_ref, group_of(i), 2)
        source = added_sources(conserved_of(prim), prim)
        cons = cons_at(i)
        done = []
        for c in range(5):
            value = cons[c] - CORR * (total[c] + (upper[c] - lower[c]))
            done.append(value + step_ratio * source[c] if c in source else value)
        sink(i, done)
        return carry

    lax.fori_loop(1, count - 1, step, 0, unroll=unroll)


def loop_scratch():
    return [
        pltpu.VMEM((4, 5 * NZ, NC), jnp.float32),
        pltpu.VMEM((2, 5 * NZ, LANES), jnp.float32),
        pltpu.VMEM((2, 5 * NZ, LANES), jnp.float32),
    ]


def prep_kernel(x_ref, xt_ref, own_ref):
    for c in range(5):
        xt_ref[:, pl.ds(c * NZ, NZ), :] = jnp.swapaxes(x_ref[pl.ds(c * NZ, NZ)], 0, 1)
    group = lanes_of((5 * NZ, LANES)) // GROUP
    packed = jnp.zeros((5 * NZ, LANES), jnp.float32)
    for row in range(NROW):
        moved = pltpu.roll(xt_ref[row], row * GROUP + GROUP // 2, 1)[:, :LANES]
        packed = jnp.where(group == row, moved, packed)
    own_ref[...] = packed


def rims_kernel(rem_ref, xt_ref, own_ref, paired_ref, crossed_ref, strip_ref, even_ref, odd_ref, end_ref):
    lane = lanes_of((5 * NZ, LANES))
    from_low = (lane % GROUP) < GROUP // 2
    own = own_ref[...]
    even = rem_ref[3] == 0
    low = jnp.where(from_low, jnp.where(even, crossed_ref[...], paired_ref[...]), own)
    high = jnp.where(from_low, own, jnp.where(even, paired_ref[...], crossed_ref[...]))
    strip_ref[:, :LANES] = low
    strip_ref[:, LANES:] = high
    three = WIDTH * GROUP
    lower = jnp.where(lane < three, low, pltpu.roll(high, three, 1))
    upper = jnp.where(lane < three, pltpu.roll(low, three, 1), pltpu.roll(high, 2 * three, 1))
    upward = jnp.bitwise_and(rem_ref[1], 1) == 0
    for ref, flag in ((even_ref, upward), (odd_ref, jnp.logical_not(upward))):
        first = jnp.where(flag, NROW - WIDTH, 0)
        ref[2 * WIDTH] = jnp.where(flag, upper, lower)
        for w in range(WIDTH):
            for side in range(2):
                ref[2 * w + side] = xt_ref[first + w, :, side * LANES : (side + 1) * LANES]

    at_low = rem_ref[1] == 0
    first = jnp.where(at_low, 0, NROW - WIDTH)
    by = jnp.where(at_low, NC - rem_ref[0], rem_ref[0])
    strips = jnp.zeros((5 * NZ, LANES), jnp.float32)
    for w in range(WIDTH):
        row = first + w
        main = xt_ref[row]
        moved = pltpu.roll(main, jnp.bitwise_and(by, NC - 1), 1)
        end_ref[2 * w] = moved[:, :LANES]
        end_ref[2 * w + 1] = moved[:, LANES:]
        above = pltpu.roll(high, jnp.bitwise_and(2 * LANES - GROUP * row - GROUP // 2, LANES - 1), 1)
        below = pltpu.roll(low, jnp.bitwise_and(2 * LANES - GROUP * row - GROUP // 2, LANES - 1), 1)
        wide = jnp.concatenate([main, above, below], axis=1)
        cut = pltpu.roll(wide, jnp.bitwise_and(by - (NC - GROUP // 2) + w * GROUP + 2 * NC, 2 * NC - 1), 1)
        strips = jnp.where(lane // GROUP == w, cut[:, :LANES], strips)
    end_ref[2 * WIDTH] = strips


def inner_kernel(xt_ref, strip_ref, out_ref, kept_ref, prim_ref, save_ref, first_ref, second_ref):
    cons = row_of(strip_ref)
    prim, speed, az = edge_faces_of(cons)
    keep_faces(first_ref, az)
    half = strip_half(cons, prim, speed, az, rolled(cons, GROUP, 1), rolled(cons, -GROUP, 1))
    keep_faces(second_ref, second_order_faces(primitive(half), 2, 1))
    predict(
        NROW,
        lambda i: row_of(xt_ref, i),
        lambda i: (first_ref, i),
        lambda i, arrays: put_row(prim_ref, i, arrays),
        save_ref,
        2,
    )
    for n in range(4):
        kept_ref[n] = prim_ref[1 + n]
        kept_ref[4 + n] = prim_ref[NROW - 5 + n]
    correct(
        NROW - 4,
        lambda i: row_of(prim_ref, i + 2),
        lambda i: row_of(xt_ref, i + 2),
        second_ref,
        lambda i: i + 2,
        lambda i, arrays: put_row(out_ref, i + 2, arrays),
        save_ref,
        2,
    )


def outer_kernel(
    rem_ref, xt_ref, strip_ref, kept_ref, even_ref, odd_ref, e1_ref, e2_ref, seen_ref, in_ref, whole_ref,
    cons_ref, prim_ref, save_ref, first_ref, second_ref, ghost_ref, strips_ref,
    out_ref, sem,
):
    del seen_ref, in_ref
    rem, rad, last = rem_ref[0], rem_ref[1], rem_ref[2]
    lane = lanes_of((5 * NZ, LANES))
    three = WIDTH * GROUP

    upward = jnp.bitwise_and(rad, 1) == 0

    def from_neighbour(seg, tile):
        flag = upward if seg else jnp.logical_not(upward)
        return jnp.where(flag, even_ref[tile], odd_ref[tile])

    def own_side(seg):
        for w in range(WIDTH):
            for side in range(2):
                cons_ref[seg, WIDTH * seg + w, :, side * LANES : (side + 1) * LANES] = from_neighbour(seg, 2 * w + side)

    def end_side(seg, upper_ref, lower_ref, cut):
        for w in range(WIDTH):
            for side in range(2):
                cons_ref[seg, WIDTH * seg + w, :, side * LANES : (side + 1) * LANES] = jnp.where(
                    lane + side * LANES >= cut, upper_ref[2 * w + side], lower_ref[2 * w + side]
                )

    @pl.when(rad != 0)
    def _():
        own_side(0)
        strips_ref[0] = from_neighbour(0, 2 * WIDTH)
        strips_ref[1] = pltpu.roll(from_neighbour(0, 2 * WIDTH), LANES - three, 1)

    @pl.when(rad == 0)
    def _():
        end_side(0, e1_ref, e2_ref, rem)
        strips_ref[0] = e2_ref[2 * WIDTH]
        strips_ref[1] = e1_ref[2 * WIDTH]

    @pl.when(rad != last)
    def _():
        own_side(1)
        strips_ref[0] = jnp.where(lane < three, strips_ref[0], pltpu.roll(from_neighbour(1, 2 * WIDTH), three, 1))
        strips_ref[1] = jnp.where(lane < three, strips_ref[1], from_neighbour(1, 2 * WIDTH))

    @pl.when(rad == last)
    def _():
        end_side(1, e2_ref, e1_ref, NC - rem)
        strips_ref[0] = jnp.where(lane < three, strips_ref[0], pltpu.roll(e1_ref[2 * WIDTH], three, 1))
        strips_ref[1] = jnp.where(lane < three, strips_ref[1], pltpu.roll(e2_ref[2 * WIDTH], three, 1))

    for w in range(WIDTH):
        cons_ref[0, WIDTH + w] = xt_ref[w]
        cons_ref[1, w] = xt_ref[NROW - WIDTH + w]
    for n in range(4):
        prim_ref[0, 3 + n] = kept_ref[n]
        prim_ref[1, n] = kept_ref[4 + n]

    ghost = [
        jnp.concatenate([strips_ref[0, pl.ds(c * NZ, NZ), :], strips_ref[1, pl.ds(c * NZ, NZ), :]], axis=1)
        for c in range(5)
    ]
    keep_faces(ghost_ref.at[0], edge_faces_of(ghost)[2])
    cons = row_of(strip_ref)
    prim, speed, az = edge_faces_of(cons)
    keep_faces(first_ref, az)
    in_tile = lanes_of((NZ, NC)) % LANES
    below = [
        jnp.where(in_tile < GROUP, a, b) for a, b in zip(rolled(ghost, -2 * GROUP, 1), rolled(cons, GROUP, 1))
    ]
    above = [
        jnp.where(in_tile >= LANES - GROUP, a, b)
        for a, b in zip(rolled(ghost, LANES - 4 * GROUP, 1), rolled(cons, -GROUP, 1))
    ]
    half = strip_half(cons, prim, speed, az, below, above)
    keep_faces(second_ref, second_order_faces(primitive(half), 2, 1))

    group = lanes_of((5 * NZ, LANES)) // GROUP
    for side in range(2):
        mine, both = first_ref[side], ghost_ref[0, side]
        ghost_ref[0, side] = jnp.where(group == 3, pltpu.roll(mine, 3 * GROUP, 1), both)
        ghost_ref[1, side] = jnp.where(group == 1, pltpu.roll(mine, 2 * GROUP, 1), pltpu.roll(both, LANES - GROUP, 1))

    def segment(seg, carry):
        predict(
            5,
            lambda i: row_of(cons_ref, seg, i + seg),
            lambda i: (ghost_ref.at[seg], i),
            lambda i, arrays: put_row(prim_ref.at[seg], i - 1 + 4 * seg, arrays),
            save_ref,
            1,
        )
        correct(
            5,
            lambda i: row_of(prim_ref, seg, i + 1),
            lambda i: row_of(cons_ref, seg, i + 2 - 3 * seg),
            second_ref,
            lambda i: i - 1 + 13 * seg,
            lambda i, arrays: put_row(out_ref.at[seg], i - 1, arrays),
            save_ref,
            1,
        )
        return carry

    lax.fori_loop(0, 2, segment, 0)
    copies = [
        pltpu.make_async_copy(out_ref.at[seg], whole_ref.at[pl.ds(seg * (NROW - WIDTH), WIDTH)], sem.at[seg])
        for seg in range(2)
    ]
    for copy in copies:
        copy.start()
    for copy in copies:
        copy.wait()


def remap_kernel(count, shift_ref, frac_ref, x_ref, o_ref):
    row = shift_ref[NROW]
    shift, frac = shift_ref[row], frac_ref[row]
    tiles = 2 * count
    hop = jnp.bitwise_and(jnp.right_shift(shift, 7), tiles - 1)
    rem = jnp.bitwise_and(shift, LANES - 1)
    lane = lanes_of((5 * NZ, LANES))
    near, far = lane >= rem, lane > rem
    rest = 1.0 - frac

    def place(k):
        start = pl.multiple_of(jnp.bitwise_and(k, 1) * LANES, LANES)
        return jnp.right_shift(k, 1), slice(None), pl.ds(start, LANES)

    def turned(k):
        tile = x_ref[place(k)]
        return pltpu.roll(tile, rem, 1), pltpu.roll(tile, jnp.bitwise_and(rem + 1, LANES - 1), 1)

    def one(k, before):
        here = turned(k)
        value = rest * jnp.where(near, here[0], before[0]) + frac * jnp.where(far, here[1], before[1])
        o_ref[place(jnp.bitwise_and(k + hop, tiles - 1))] = value
        return here

    lax.fori_loop(0, tiles, one, turned(jnp.int32(tiles - 1)), unroll=2)


def finish_kernel(y_ref, o_ref):
    for c in range(5):
        o_ref[pl.ds(c * NZ, NZ)] = jnp.swapaxes(y_ref[:, pl.ds(c * NZ, NZ), :], 0, 1)


def shape(*dims):
    return jax.ShapeDtypeStruct(dims, jnp.float32)


def local(conserved, shift_cells, shift_frac, boundary_offset):
    azs, rads = lax.axis_size("az"), lax.axis_size("rad")
    az, rad = lax.axis_index("az"), lax.axis_index("rad")
    offset = boundary_offset[0]
    hop, rem = offset // NC, offset % NC
    scalars = jnp.stack([rem, rad, jnp.int32(rads - 1), az % 2]).astype(jnp.int32)
    row_shape, strip_shape = (5 * NZ, NC), (5 * NZ, LANES)
    rows, own = pl.pallas_call(
        prep_kernel,
        out_shape=(shape(NROW, *row_shape), shape(*strip_shape)),
        in_specs=[VMEM],
        out_specs=(VMEM,) * 2,
        compiler_params=PARAMS,
    )(conserved.reshape(5 * NZ, NROW, NC))
    paired = lax.ppermute(own, "az", [(i, i ^ 1) for i in range(azs)])
    crossed = lax.ppermute(own, "az", [(i, (i + 1 if i % 2 else i - 1) % azs) for i in range(azs)])
    rim = shape(2 * WIDTH + 1, *strip_shape)
    strip, even, odd, end = pl.pallas_call(
        rims_kernel,
        out_shape=(shape(*row_shape), rim, rim, rim),
        in_specs=[SMEM] + [VMEM] * 4,
        out_specs=(VMEM,) * 4,
        compiler_params=PARAMS,
    )(scalars, rows, own, paired, crossed)
    scratch = loop_scratch()

    def inner(rows, strip):
        return pl.pallas_call(
            inner_kernel,
            out_shape=(shape(NROW, *row_shape), shape(8, *row_shape)),
            in_specs=[VMEM] * 2,
            out_specs=(VMEM,) * 2,
            scratch_shapes=[pltpu.VMEM((NROW, *row_shape), jnp.float32), *scratch],
            compiler_params=PARAMS,
            cost_estimate=pl.CostEstimate(flops=30 * 10**6, bytes_accessed=4 * 2**20, transcendentals=0),
        )(rows, strip)

    def ends(k):
        pairs = [(a * rads + rads - 1, (a + k) % azs * rads) for a in range(azs)]
        return pairs + [(b, a) for a, b in pairs]

    def moved_by(k):
        def send(block, even, odd, rows, strip):
            even = lax.ppermute(even, "rad", [(i, i ^ 1) for i in range(rads)])
            odd = lax.ppermute(odd, "rad", [(i, i + 1 if i % 2 else i - 1) for i in range(1, rads - 1)])
            first, second = (lax.ppermute(block, ("az", "rad"), ends(j % azs)) for j in (k, k + 1))
            seen = first[-1, :8] + second[-1, :8]
            return first, second, even, odd, seen, *inner(rows, strip)

        return send

    first, second, even, odd, seen, updated, kept = lax.switch(
        hop, [moved_by(k) for k in range(azs)], end, even, odd, rows, strip
    )
    updated = pl.pallas_call(
        outer_kernel,
        out_shape=shape(NROW, *row_shape),
        in_specs=[SMEM] + [VMEM] * 7 + [ANY] * 2,
        out_specs=ANY,
        input_output_aliases={9: 0},
        scratch_shapes=[
            pltpu.VMEM((2, 6, *row_shape), jnp.float32),
            pltpu.VMEM((2, 7, *row_shape), jnp.float32),
            *scratch,
            pltpu.VMEM((2, 2, *strip_shape), jnp.float32),
            pltpu.VMEM((2, *strip_shape), jnp.float32),
            pltpu.VMEM((2, WIDTH, *row_shape), jnp.float32),
            pltpu.SemaphoreType.DMA((2,)),
        ],
        compiler_params=PARAMS,
    )(scalars, rows, strip, kept, even, odd, first, second, seen, updated)

    whole_row = lax.all_to_all(updated, "az", 0, 0, tiled=True)
    shifts = jnp.concatenate([shift_cells, az[None].astype(jnp.int32)])
    moved = pl.pallas_call(
        functools.partial(remap_kernel, azs),
        out_shape=shape(azs, *row_shape),
        in_specs=[SMEM, SMEM, VMEM],
        out_specs=VMEM,
        compiler_params=PARAMS,
    )(shifts, shift_frac, whole_row)
    back = lax.all_to_all(moved, "az", 0, 0, tiled=True)
    result = pl.pallas_call(
        finish_kernel,
        out_shape=shape(5 * NZ, NROW, NC),
        in_specs=[VMEM],
        out_specs=VMEM,
        compiler_params=PARAMS,
    )(back)
    return result.reshape(5, NZ, NROW, NC)


def solution(mesh):
    in_specs = (P(None, None, "rad", "az"), P("rad"), P("rad"), P())
    out_specs = P(None, None, "rad", "az")
    return jax.shard_map(local, mesh=mesh, in_specs=in_specs, out_specs=out_specs, check_vma=False)
```

```python
import functools

import jax
import jax.numpy as jnp
from jax import lax
from jax.experimental import pallas as pl
from jax.experimental.pallas import tpu as pltpu
from jax.sharding import PartitionSpec as P

gamma_ratio = 5.0 / 3.0
step_ratio = 0.06
omega_rate = 1.0
shear_rate = 1.5

NZ = 16
NROW = 16
NC = 256
LANES = 128
WIDTH = 3
PRED = 0.25 * step_ratio
CORR = 0.5 * step_ratio
GROUP = 8
VMEM = pl.BlockSpec(memory_space=pltpu.VMEM)
ANY = pl.BlockSpec(memory_space=pl.ANY)
SMEM = pl.BlockSpec(memory_space=pltpu.SMEM)
PARAMS = pltpu.CompilerParams(vmem_limit_bytes=48 * 2**20)


def lanes_of(shape):
    return lax.broadcasted_iota(jnp.int32, shape, len(shape) - 1)


def reciprocal(x):
    guess = pl.reciprocal(x, approx=True)
    return guess * (2.0 - x * guess)


def primitive(cons):
    inverse = reciprocal(cons[0])
    vel = [cons[n] * inverse for n in (1, 2, 3)]
    kinetic = 0.5 * (cons[1] * vel[0] + cons[2] * vel[1] + cons[3] * vel[2])
    return [cons[0], *vel, (gamma_ratio - 1.0) * (cons[4] - kinetic)]


def conserved_of(prim):
    mom = [prim[0] * prim[n] for n in (1, 2, 3)]
    kinetic = 0.5 * (mom[0] * prim[1] + mom[1] * prim[2] + mom[2] * prim[3])
    return [prim[0], *mom, prim[4] * (1.0 / (gamma_ratio - 1.0)) + kinetic]


def sound(prim):
    scaled = gamma_ratio * prim[4]
    return scaled * lax.rsqrt(scaled * prim[0])


def flux_of(prim, cons, normal):
    speed = prim[normal]
    flux = [cons[normal]]
    for n in (1, 2, 3):
        term = cons[n] * speed
        flux.append(term + prim[4] if n == normal else term)
    flux.append((cons[4] + prim[4]) * speed)
    return flux


def twice_face(low_flux, low_cons, low_reach, flux, cons, reach):
    top = jnp.maximum(low_reach, reach)
    return [(a + b) - top * (v - u) for a, b, u, v in zip(low_flux, flux, low_cons, cons)]


def minmod(a, b):
    return jnp.maximum(jnp.minimum(a, b), 0.0) + jnp.minimum(jnp.maximum(a, b), 0.0)


def rolled(arrays, by, axis):
    return [pltpu.roll(x, by % x.shape[axis], axis) for x in arrays]


def first_order_faces(prim, cons, speed_of_sound, normal, axis):
    flux = flux_of(prim, cons, normal)
    reach = jnp.abs(prim[normal]) + speed_of_sound
    low_cons = rolled(cons, 1, axis)
    low_flux = [low_cons[normal], *rolled(flux[1:], 1, axis)]
    low_reach = pltpu.roll(reach, 1, axis)
    return twice_face(low_flux, low_cons, low_reach, flux, cons, reach)


def state_at(prim, normal):
    cons = conserved_of(prim)
    return flux_of(prim, cons, normal), cons, jnp.abs(prim[normal]) + sound(prim)


def second_order_faces(prim, normal, axis):
    diff = [x - y for x, y in zip(prim, rolled(prim, 1, axis))]
    half_slope = [0.5 * minmod(a, b) for a, b in zip(diff, rolled(diff, -1, axis))]
    low = rolled([x + s for x, s in zip(prim, half_slope)], 1, axis)
    high = [x - s for x, s in zip(prim, half_slope)]
    return twice_face(*state_at(low, normal), *state_at(high, normal))


def added_sources(cons, prim):
    return {
        1: 2.0 * omega_rate * cons[2],
        2: -(2.0 - shear_rate) * omega_rate * cons[1],
        4: shear_rate * omega_rate * cons[1] * prim[2],
    }


def row_of(ref, *index):
    return [ref[(*index, pl.ds(c * NZ, NZ), slice(None))] for c in range(5)]


def put_row(ref, index, arrays):
    for c in range(5):
        ref[index, pl.ds(c * NZ, NZ), :] = arrays[c]


def tile_lanes():
    return lanes_of((NZ, LANES))


def edge_faces_of(strip):
    prim = primitive(strip)
    speed = sound(prim)
    return prim, speed, first_order_faces(prim, strip, speed, 2, 1)


def keep_faces(ref, faces):
    for c in range(5):
        for side in range(2):
            ref[side, pl.ds(c * NZ, NZ), :] = faces[c][:, side * LANES : (side + 1) * LANES]


def strip_half(cons, prim, speed, az, below, above):
    def rad_state(u):
        q = primitive(u)
        return flux_of(q, u, 1), u, jnp.abs(q[1]) + sound(q)

    mid_state = (flux_of(prim, cons, 1), cons, jnp.abs(prim[1]) + speed)
    rad_low = twice_face(*rad_state(below), *mid_state)
    rad_high = twice_face(*mid_state, *rad_state(above))
    vert = first_order_faces(prim, cons, speed, 3, 0)
    source = added_sources(cons, prim)
    half = []
    for c in range(5):
        total = (rad_high[c] - rad_low[c]) + (pltpu.roll(az[c], NC - 1, 1) - az[c])
        total = total + (pltpu.roll(vert[c], NZ - 1, 0) - vert[c])
        value = cons[c] - PRED * total
        half.append(value + 0.5 * step_ratio * source[c] if c in source else value)
    return half


def patched(faces, faces_ref, group, count):
    lane = tile_lanes()
    lower, upper = [], []
    for c in range(5):
        rows = pl.ds(c * NZ, NZ)
        at_edge = (2 * LANES - GROUP * group - GROUP // 2) % LANES
        before_edge = (3 * LANES - 1 - GROUP * group - GROUP // 2) % LANES
        left = pltpu.roll(faces_ref[0, rows, :], at_edge, 1)
        tiles = [jnp.where(lane < count, left, faces[c][:, :LANES]), faces[c][:, LANES:]]
        right = faces_ref[1, rows, :]
        beyond = pltpu.roll(right, before_edge, 1)
        if count > 1:
            tiles[1] = jnp.where(lane == LANES - 1, pltpu.roll(right, at_edge, 1), tiles[1])
        whole = jnp.concatenate(tiles, axis=1)
        lower.append(whole)
        above = pltpu.roll(whole, NC - 1, 1)
        last = jnp.where(lane == LANES - 1, beyond, above[:, LANES:])
        upper.append(jnp.concatenate([above[:, :LANES], last], axis=1))
    return lower, upper


def predict(count, tracks, unroll):
    def state(load, i):
        cons = load(i)
        prim = primitive(cons)
        speed = sound(prim)
        return prim, speed, (flux_of(prim, cons, 1), cons, jnp.abs(prim[1]) + speed)

    def keep(save_ref, prim, speed, rad_state, rad):
        put_row(save_ref, 0, rad_state[0])
        put_row(save_ref, 1, rad)
        put_row(save_ref, 2, prim)
        save_ref[3, pl.ds(0, NZ), :] = speed
        save_ref[3, pl.ds(NZ, NZ), :] = rad_state[2]

    for load, _, _, save_ref in tracks:
        before = state(load, 0)[2]
        prim, speed, here = state(load, 1)
        keep(save_ref, prim, speed, here, twice_face(*before, *here))

    def one(i, load, faces_at, sink, save_ref):
        cons = load(i)
        low = row_of(save_ref, 1)
        prim = row_of(save_ref, 2)
        speed = save_ref[3, pl.ds(0, NZ), :]
        here = (row_of(save_ref, 0), cons, save_ref[3, pl.ds(NZ, NZ), :])
        next_prim, next_speed, there = state(load, i + 1)
        rad = twice_face(*here, *there)
        keep(save_ref, next_prim, next_speed, there, rad)
        total = [x - y for x, y in zip(rad, low)]
        vert = first_order_faces(prim, cons, speed, 3, 0)
        total = [t + (pltpu.roll(x, NZ - 1, 0) - x) for t, x in zip(total, vert)]
        lower, upper = patched(first_order_faces(prim, cons, speed, 2, 1), *faces_at(i), 1)
        source = added_sources(cons, prim)
        half = []
        for c in range(5):
            value = cons[c] - PRED * (total[c] + (upper[c] - lower[c]))
            half.append(value + 0.5 * step_ratio * source[c] if c in source else value)
        sink(i, primitive(half))

    def step(i, carry):
        for track in tracks:
            one(i, *track)
        return carry

    lax.fori_loop(1, count - 1, step, 0, unroll=unroll)


def correct(count, tracks, unroll):
    def sides(load, i):
        prim = load(i)
        half_slope = [0.5 * minmod(x - a, b - x) for x, a, b in zip(prim, load(i - 1), load(i + 1))]
        return [x - s for x, s in zip(prim, half_slope)], [x + s for x, s in zip(prim, half_slope)]

    for load, *_, save_ref in tracks:
        above = sides(load, 0)[1]
        high, upper_side = sides(load, 1)
        put_row(save_ref, 0, upper_side)
        put_row(save_ref, 1, twice_face(*state_at(above, 1), *state_at(high, 1)))

    def one(i, load, cons_at, faces_ref, group_of, sink, save_ref):
        below = row_of(save_ref, 0)
        low = row_of(save_ref, 1)
        high, upper_side = sides(load, i + 1)
        rad = twice_face(*state_at(below, 1), *state_at(high, 1))
        put_row(save_ref, 0, upper_side)
        put_row(save_ref, 1, rad)
        total = [x - y for x, y in zip(rad, low)]
        prim = load(i)
        vert = second_order_faces(prim, 3, 0)
        total = [t + (pltpu.roll(x, NZ - 1, 0) - x) for t, x in zip(total, vert)]
        lower, upper = patched(second_order_faces(prim, 2, 1), faces_ref, group_of(i), 2)
        source = added_sources(conserved_of(prim), prim)
        cons = cons_at(i)
        done = []
        for c in range(5):
            value = cons[c] - CORR * (total[c] + (upper[c] - lower[c]))
            done.append(value + step_ratio * source[c] if c in source else value)
        sink(i, done)

    def step(i, carry):
        for track in tracks:
            one(i, *track)
        return carry

    lax.fori_loop(1, count - 1, step, 0, unroll=unroll)


def loop_scratch():
    return [
        pltpu.VMEM((8, 5 * NZ, NC), jnp.float32),
        pltpu.VMEM((2, 5 * NZ, LANES), jnp.float32),
        pltpu.VMEM((2, 5 * NZ, LANES), jnp.float32),
    ]


def prep_kernel(x_ref, xt_ref, own_ref):
    for c in range(5):
        xt_ref[:, pl.ds(c * NZ, NZ), :] = jnp.swapaxes(x_ref[pl.ds(c * NZ, NZ)], 0, 1)
    group = lanes_of((5 * NZ, LANES)) // GROUP
    packed = jnp.zeros((5 * NZ, LANES), jnp.float32)
    for row in range(NROW):
        moved = pltpu.roll(xt_ref[row], row * GROUP + GROUP // 2, 1)[:, :LANES]
        packed = jnp.where(group == row, moved, packed)
    own_ref[...] = packed


def rims_kernel(rem_ref, xt_ref, own_ref, paired_ref, crossed_ref, strip_ref, even_ref, odd_ref, end_ref):
    lane = lanes_of((5 * NZ, LANES))
    from_low = (lane % GROUP) < GROUP // 2
    own = own_ref[...]
    even = rem_ref[3] == 0
    low = jnp.where(from_low, jnp.where(even, crossed_ref[...], paired_ref[...]), own)
    high = jnp.where(from_low, own, jnp.where(even, paired_ref[...], crossed_ref[...]))
    strip_ref[:, :LANES] = low
    strip_ref[:, LANES:] = high
    three = WIDTH * GROUP
    lower = jnp.where(lane < three, low, pltpu.roll(high, three, 1))
    upper = jnp.where(lane < three, pltpu.roll(low, three, 1), pltpu.roll(high, 2 * three, 1))
    upward = jnp.bitwise_and(rem_ref[1], 1) == 0
    for ref, flag in ((even_ref, upward), (odd_ref, jnp.logical_not(upward))):
        first = jnp.where(flag, NROW - WIDTH, 0)
        ref[2 * WIDTH] = jnp.where(flag, upper, lower)
        for w in range(WIDTH):
            for side in range(2):
                ref[2 * w + side] = xt_ref[first + w, :, side * LANES : (side + 1) * LANES]

    at_low = rem_ref[1] == 0
    first = jnp.where(at_low, 0, NROW - WIDTH)
    by = jnp.where(at_low, NC - rem_ref[0], rem_ref[0])
    strips = jnp.zeros((5 * NZ, LANES), jnp.float32)
    for w in range(WIDTH):
        row = first + w
        main = xt_ref[row]
        moved = pltpu.roll(main, jnp.bitwise_and(by, NC - 1), 1)
        end_ref[2 * w] = moved[:, :LANES]
        end_ref[2 * w + 1] = moved[:, LANES:]
        above = pltpu.roll(high, jnp.bitwise_and(2 * LANES - GROUP * row - GROUP // 2, LANES - 1), 1)
        below = pltpu.roll(low, jnp.bitwise_and(2 * LANES - GROUP * row - GROUP // 2, LANES - 1), 1)
        wide = jnp.concatenate([main, above, below], axis=1)
        cut = pltpu.roll(wide, jnp.bitwise_and(by - (NC - GROUP // 2) + w * GROUP + 2 * NC, 2 * NC - 1), 1)
        strips = jnp.where(lane // GROUP == w, cut[:, :LANES], strips)
    end_ref[2 * WIDTH] = strips


def inner_kernel(xt_ref, strip_ref, out_ref, kept_ref, prim_ref, save_ref, first_ref, second_ref):
    cons = row_of(strip_ref)
    prim, speed, az = edge_faces_of(cons)
    keep_faces(first_ref, az)
    half = strip_half(cons, prim, speed, az, rolled(cons, GROUP, 1), rolled(cons, -GROUP, 1))
    keep_faces(second_ref, second_order_faces(primitive(half), 2, 1))
    track = (
        lambda i: row_of(xt_ref, i),
        lambda i: (first_ref, i),
        lambda i, arrays: put_row(prim_ref, i, arrays),
        save_ref,
    )
    predict(NROW, [track], 1)
    for n in range(4):
        kept_ref[n] = prim_ref[1 + n]
        kept_ref[4 + n] = prim_ref[NROW - 5 + n]
    track = (
        lambda i: row_of(prim_ref, i + 2),
        lambda i: row_of(xt_ref, i + 2),
        second_ref,
        lambda i: i + 2,
        lambda i, arrays: put_row(out_ref, i + 2, arrays),
        save_ref,
    )
    correct(NROW - 4, [track], 2)


def outer_kernel(
    rem_ref, xt_ref, strip_ref, kept_ref, even_ref, odd_ref, e1_ref, e2_ref, seen_ref, in_ref, whole_ref,
    cons_ref, prim_ref, save_ref, first_ref, second_ref, ghost_ref, strips_ref,
    out_ref, sem,
):
    del seen_ref, in_ref
    rem, rad, last = rem_ref[0], rem_ref[1], rem_ref[2]
    lane = lanes_of((5 * NZ, LANES))
    three = WIDTH * GROUP

    upward = jnp.bitwise_and(rad, 1) == 0

    def from_neighbour(seg, tile):
        flag = upward if seg else jnp.logical_not(upward)
        return jnp.where(flag, even_ref[tile], odd_ref[tile])

    def own_side(seg):
        for w in range(WIDTH):
            for side in range(2):
                cons_ref[seg, WIDTH * seg + w, :, side * LANES : (side + 1) * LANES] = from_neighbour(seg, 2 * w + side)

    def end_side(seg, upper_ref, lower_ref, cut):
        for w in range(WIDTH):
            for side in range(2):
                cons_ref[seg, WIDTH * seg + w, :, side * LANES : (side + 1) * LANES] = jnp.where(
                    lane + side * LANES >= cut, upper_ref[2 * w + side], lower_ref[2 * w + side]
                )

    @pl.when(rad != 0)
    def _():
        own_side(0)
        strips_ref[0] = from_neighbour(0, 2 * WIDTH)
        strips_ref[1] = pltpu.roll(from_neighbour(0, 2 * WIDTH), LANES - three, 1)

    @pl.when(rad == 0)
    def _():
        end_side(0, e1_ref, e2_ref, rem)
        strips_ref[0] = e2_ref[2 * WIDTH]
        strips_ref[1] = e1_ref[2 * WIDTH]

    @pl.when(rad != last)
    def _():
        own_side(1)
        strips_ref[0] = jnp.where(lane < three, strips_ref[0], pltpu.roll(from_neighbour(1, 2 * WIDTH), three, 1))
        strips_ref[1] = jnp.where(lane < three, strips_ref[1], from_neighbour(1, 2 * WIDTH))

    @pl.when(rad == last)
    def _():
        end_side(1, e2_ref, e1_ref, NC - rem)
        strips_ref[0] = jnp.where(lane < three, strips_ref[0], pltpu.roll(e1_ref[2 * WIDTH], three, 1))
        strips_ref[1] = jnp.where(lane < three, strips_ref[1], pltpu.roll(e2_ref[2 * WIDTH], three, 1))

    for w in range(WIDTH):
        cons_ref[0, WIDTH + w] = xt_ref[w]
        cons_ref[1, w] = xt_ref[NROW - WIDTH + w]
    for n in range(4):
        prim_ref[0, 3 + n] = kept_ref[n]
        prim_ref[1, n] = kept_ref[4 + n]

    ghost = [
        jnp.concatenate([strips_ref[0, pl.ds(c * NZ, NZ), :], strips_ref[1, pl.ds(c * NZ, NZ), :]], axis=1)
        for c in range(5)
    ]
    keep_faces(ghost_ref.at[0], edge_faces_of(ghost)[2])
    cons = row_of(strip_ref)
    prim, speed, az = edge_faces_of(cons)
    keep_faces(first_ref, az)
    in_tile = lanes_of((NZ, NC)) % LANES
    below = [
        jnp.where(in_tile < GROUP, a, b) for a, b in zip(rolled(ghost, -2 * GROUP, 1), rolled(cons, GROUP, 1))
    ]
    above = [
        jnp.where(in_tile >= LANES - GROUP, a, b)
        for a, b in zip(rolled(ghost, LANES - 4 * GROUP, 1), rolled(cons, -GROUP, 1))
    ]
    half = strip_half(cons, prim, speed, az, below, above)
    keep_faces(second_ref, second_order_faces(primitive(half), 2, 1))

    group = lanes_of((5 * NZ, LANES)) // GROUP
    for side in range(2):
        mine, both = first_ref[side], ghost_ref[0, side]
        ghost_ref[0, side] = jnp.where(group == 3, pltpu.roll(mine, 3 * GROUP, 1), both)
        ghost_ref[1, side] = jnp.where(group == 1, pltpu.roll(mine, 2 * GROUP, 1), pltpu.roll(both, LANES - GROUP, 1))

    def predicted(seg):
        return (
            lambda i: row_of(cons_ref, seg, i + seg),
            lambda i: (ghost_ref.at[seg], i),
            lambda i, arrays: put_row(prim_ref.at[seg], i - 1 + 4 * seg, arrays),
            save_ref.at[pl.ds(4 * seg, 4)],
        )

    def corrected(seg):
        return (
            lambda i: row_of(prim_ref, seg, i + 1),
            lambda i: row_of(cons_ref, seg, i + 2 - 3 * seg),
            second_ref,
            lambda i: i - 1 + 13 * seg,
            lambda i, arrays: put_row(out_ref.at[seg], i - 1, arrays),
            save_ref.at[pl.ds(4 * seg, 4)],
        )

    predict(5, [predicted(0), predicted(1)], 1)
    correct(5, [corrected(0), corrected(1)], 1)
    copies = [
        pltpu.make_async_copy(out_ref.at[seg], whole_ref.at[pl.ds(seg * (NROW - WIDTH), WIDTH)], sem.at[seg])
        for seg in range(2)
    ]
    for copy in copies:
        copy.start()
    for copy in copies:
        copy.wait()


def remap_kernel(count, turn_ref, x_ref, o_ref):
    shift, frac = turn_ref[0].astype(jnp.int32), turn_ref[1]
    tiles = 2 * count
    hop = jnp.bitwise_and(jnp.right_shift(shift, 7), tiles - 1)
    rem = jnp.bitwise_and(shift, LANES - 1)
    lane = lanes_of((5 * NZ, LANES))
    near, far = lane >= rem, lane > rem
    rest = 1.0 - frac

    def place(k):
        start = pl.multiple_of(jnp.bitwise_and(k, 1) * LANES, LANES)
        return jnp.right_shift(k, 1), slice(None), pl.ds(start, LANES)

    def turned(k):
        tile = x_ref[place(k)]
        return pltpu.roll(tile, rem, 1), pltpu.roll(tile, jnp.bitwise_and(rem + 1, LANES - 1), 1)

    def one(k, before):
        here = turned(k)
        value = rest * jnp.where(near, here[0], before[0]) + frac * jnp.where(far, here[1], before[1])
        o_ref[place(jnp.bitwise_and(k + hop, tiles - 1))] = value
        return here

    lax.fori_loop(0, tiles, one, turned(jnp.int32(tiles - 1)), unroll=2)


def finish_kernel(y_ref, o_ref):
    for c in range(5):
        o_ref[pl.ds(c * NZ, NZ)] = jnp.swapaxes(y_ref[:, pl.ds(c * NZ, NZ), :], 0, 1)


def shape(*dims):
    return jax.ShapeDtypeStruct(dims, jnp.float32)


def local(conserved, shift_cells, shift_frac, boundary_offset):
    azs, rads = lax.axis_size("az"), lax.axis_size("rad")
    az, rad = lax.axis_index("az"), lax.axis_index("rad")
    offset = boundary_offset[0]
    hop, rem = offset // NC, offset % NC
    scalars = jnp.stack([rem, rad, jnp.int32(rads - 1), az % 2]).astype(jnp.int32)
    row_shape, strip_shape = (5 * NZ, NC), (5 * NZ, LANES)
    rows, own = pl.pallas_call(
        prep_kernel,
        out_shape=(shape(NROW, *row_shape), shape(*strip_shape)),
        in_specs=[VMEM],
        out_specs=(VMEM,) * 2,
        compiler_params=PARAMS,
    )(conserved.reshape(5 * NZ, NROW, NC))
    paired = lax.ppermute(own, "az", [(i, i ^ 1) for i in range(azs)])
    crossed = lax.ppermute(own, "az", [(i, (i + 1 if i % 2 else i - 1) % azs) for i in range(azs)])
    rim = shape(2 * WIDTH + 1, *strip_shape)
    strip, even, odd, end = pl.pallas_call(
        rims_kernel,
        out_shape=(shape(*row_shape), rim, rim, rim),
        in_specs=[SMEM] + [VMEM] * 4,
        out_specs=(VMEM,) * 4,
        compiler_params=PARAMS,
    )(scalars, rows, own, paired, crossed)
    row_shift = lax.dynamic_slice_in_dim(shift_cells, az, 1)
    row_frac = lax.dynamic_slice_in_dim(shift_frac, az, 1)
    turn = jnp.concatenate([row_shift.astype(jnp.float32), row_frac])
    strip, turn = lax.optimization_barrier((strip, turn))

    scratch = loop_scratch()

    def inner(rows, strip):
        return pl.pallas_call(
            inner_kernel,
            out_shape=(shape(NROW, *row_shape), shape(8, *row_shape)),
            in_specs=[VMEM] * 2,
            out_specs=(VMEM,) * 2,
            scratch_shapes=[pltpu.VMEM((NROW, *row_shape), jnp.float32), *scratch],
            compiler_params=PARAMS,
            cost_estimate=pl.CostEstimate(flops=30 * 10**6, bytes_accessed=4 * 2**20, transcendentals=0),
        )(rows, strip)

    def ends(k):
        pairs = [(a * rads + rads - 1, (a + k) % azs * rads) for a in range(azs)]
        return pairs + [(b, a) for a, b in pairs]

    def moved_by(k):
        def send(block, even, odd, rows, strip):
            even = lax.ppermute(even, "rad", [(i, i ^ 1) for i in range(rads)])
            odd = lax.ppermute(odd, "rad", [(i, i + 1 if i % 2 else i - 1) for i in range(1, rads - 1)])
            first, second = (lax.ppermute(block, ("az", "rad"), ends(j % azs)) for j in (k, k + 1))
            seen = first[-1, :8] + second[-1, :8]
            return first, second, even, odd, seen, *inner(rows, strip)

        return send

    first, second, even, odd, seen, updated, kept = lax.switch(
        hop, [moved_by(k) for k in range(azs)], end, even, odd, rows, strip
    )
    updated = pl.pallas_call(
        outer_kernel,
        out_shape=shape(NROW, *row_shape),
        in_specs=[SMEM] + [VMEM] * 7 + [ANY] * 2,
        out_specs=ANY,
        input_output_aliases={9: 0},
        scratch_shapes=[
            pltpu.VMEM((2, 6, *row_shape), jnp.float32),
            pltpu.VMEM((2, 7, *row_shape), jnp.float32),
            *scratch,
            pltpu.VMEM((2, 2, *strip_shape), jnp.float32),
            pltpu.VMEM((2, *strip_shape), jnp.float32),
            pltpu.VMEM((2, WIDTH, *row_shape), jnp.float32),
            pltpu.SemaphoreType.DMA((2,)),
        ],
        compiler_params=PARAMS,
    )(scalars, rows, strip, kept, even, odd, first, second, seen, updated)

    whole_row = lax.all_to_all(updated, "az", 0, 0, tiled=True)
    moved = pl.pallas_call(
        functools.partial(remap_kernel, azs),
        out_shape=shape(azs, *row_shape),
        in_specs=[SMEM, VMEM],
        out_specs=VMEM,
        compiler_params=PARAMS,
    )(turn, whole_row)
    back = lax.all_to_all(moved, "az", 0, 0, tiled=True)
    result = pl.pallas_call(
        finish_kernel,
        out_shape=shape(5 * NZ, NROW, NC),
        in_specs=[VMEM],
        out_specs=VMEM,
        compiler_params=PARAMS,
    )(back)
    return result.reshape(5, NZ, NROW, NC)


def solution(mesh):
    in_specs = (P(None, None, "rad", "az"), P("rad"), P("rad"), P())
    out_specs = P(None, None, "rad", "az")
    return jax.shard_map(local, mesh=mesh, in_specs=in_specs, out_specs=out_specs, check_vma=False)
```

```python
import functools

import jax
import jax.numpy as jnp
from jax import lax
from jax.experimental import pallas as pl
from jax.experimental.pallas import tpu as pltpu
from jax.sharding import PartitionSpec as P

gamma_ratio = 5.0 / 3.0
step_ratio = 0.06
omega_rate = 1.0
shear_rate = 1.5

NZ = 16
NROW = 16
NC = 256
LANES = 128
WIDTH = 3
PRED = 0.25 * step_ratio
CORR = 0.5 * step_ratio
GROUP = 8
VMEM = pl.BlockSpec(memory_space=pltpu.VMEM)
ANY = pl.BlockSpec(memory_space=pl.ANY)
SMEM = pl.BlockSpec(memory_space=pltpu.SMEM)
PARAMS = pltpu.CompilerParams(vmem_limit_bytes=48 * 2**20)


def lanes_of(shape):
    return lax.broadcasted_iota(jnp.int32, shape, len(shape) - 1)


def reciprocal(x):
    guess = pl.reciprocal(x, approx=True)
    return guess * (2.0 - x * guess)


def primitive(cons):
    inverse = reciprocal(cons[0])
    vel = [cons[n] * inverse for n in (1, 2, 3)]
    kinetic = 0.5 * (cons[1] * vel[0] + cons[2] * vel[1] + cons[3] * vel[2])
    return [cons[0], *vel, (gamma_ratio - 1.0) * (cons[4] - kinetic)]


def conserved_of(prim):
    mom = [prim[0] * prim[n] for n in (1, 2, 3)]
    kinetic = 0.5 * (mom[0] * prim[1] + mom[1] * prim[2] + mom[2] * prim[3])
    return [prim[0], *mom, prim[4] * (1.0 / (gamma_ratio - 1.0)) + kinetic]


def sound(prim):
    scaled = gamma_ratio * prim[4]
    return scaled * lax.rsqrt(scaled * prim[0])


def flux_of(prim, cons, normal):
    speed = prim[normal]
    flux = [cons[normal]]
    for n in (1, 2, 3):
        term = cons[n] * speed
        flux.append(term + prim[4] if n == normal else term)
    flux.append((cons[4] + prim[4]) * speed)
    return flux


def twice_face(low_flux, low_cons, low_reach, flux, cons, reach):
    top = jnp.maximum(low_reach, reach)
    return [(a + b) - top * (v - u) for a, b, u, v in zip(low_flux, flux, low_cons, cons)]


def minmod(a, b):
    return jnp.maximum(jnp.minimum(a, b), 0.0) + jnp.minimum(jnp.maximum(a, b), 0.0)


def rolled(arrays, by, axis):
    return [pltpu.roll(x, by % x.shape[axis], axis) for x in arrays]


def first_order_faces(prim, cons, speed_of_sound, normal, axis):
    flux = flux_of(prim, cons, normal)
    reach = jnp.abs(prim[normal]) + speed_of_sound
    low_cons = rolled(cons, 1, axis)
    low_flux = [low_cons[normal], *rolled(flux[1:], 1, axis)]
    low_reach = pltpu.roll(reach, 1, axis)
    return twice_face(low_flux, low_cons, low_reach, flux, cons, reach)


def state_at(prim, normal):
    cons = conserved_of(prim)
    return flux_of(prim, cons, normal), cons, jnp.abs(prim[normal]) + sound(prim)


def second_order_faces(prim, normal, axis):
    diff = [x - y for x, y in zip(prim, rolled(prim, 1, axis))]
    half_slope = [0.5 * minmod(a, b) for a, b in zip(diff, rolled(diff, -1, axis))]
    low = rolled([x + s for x, s in zip(prim, half_slope)], 1, axis)
    high = [x - s for x, s in zip(prim, half_slope)]
    return twice_face(*state_at(low, normal), *state_at(high, normal))


def added_sources(cons, prim):
    return {
        1: 2.0 * omega_rate * cons[2],
        2: -(2.0 - shear_rate) * omega_rate * cons[1],
        4: shear_rate * omega_rate * cons[1] * prim[2],
    }


def row_of(ref, *index):
    return [ref[(*index, pl.ds(c * NZ, NZ), slice(None))] for c in range(5)]


def put_row(ref, index, arrays):
    for c in range(5):
        ref[index, pl.ds(c * NZ, NZ), :] = arrays[c]


def tile_lanes():
    return lanes_of((NZ, LANES))


def edge_faces_of(strip):
    prim = primitive(strip)
    speed = sound(prim)
    return prim, speed, first_order_faces(prim, strip, speed, 2, 1)


def keep_faces(ref, faces):
    for c in range(5):
        for side in range(2):
            ref[side, pl.ds(c * NZ, NZ), :] = faces[c][:, side * LANES : (side + 1) * LANES]


def strip_half(cons, prim, speed, az, below, above):
    def rad_state(u):
        q = primitive(u)
        return flux_of(q, u, 1), u, jnp.abs(q[1]) + sound(q)

    mid_state = (flux_of(prim, cons, 1), cons, jnp.abs(prim[1]) + speed)
    rad_low = twice_face(*rad_state(below), *mid_state)
    rad_high = twice_face(*mid_state, *rad_state(above))
    vert = first_order_faces(prim, cons, speed, 3, 0)
    source = added_sources(cons, prim)
    half = []
    for c in range(5):
        total = (rad_high[c] - rad_low[c]) + (pltpu.roll(az[c], NC - 1, 1) - az[c])
        total = total + (pltpu.roll(vert[c], NZ - 1, 0) - vert[c])
        value = cons[c] - PRED * total
        half.append(value + 0.5 * step_ratio * source[c] if c in source else value)
    return half


def patched(faces, faces_ref, group, count):
    lane = tile_lanes()
    lower, upper = [], []
    for c in range(5):
        rows = pl.ds(c * NZ, NZ)
        at_edge = (2 * LANES - GROUP * group - GROUP // 2) % LANES
        before_edge = (3 * LANES - 1 - GROUP * group - GROUP // 2) % LANES
        left = pltpu.roll(faces_ref[0, rows, :], at_edge, 1)
        tiles = [jnp.where(lane < count, left, faces[c][:, :LANES]), faces[c][:, LANES:]]
        right = faces_ref[1, rows, :]
        beyond = pltpu.roll(right, before_edge, 1)
        if count > 1:
            tiles[1] = jnp.where(lane == LANES - 1, pltpu.roll(right, at_edge, 1), tiles[1])
        whole = jnp.concatenate(tiles, axis=1)
        lower.append(whole)
        above = pltpu.roll(whole, NC - 1, 1)
        last = jnp.where(lane == LANES - 1, beyond, above[:, LANES:])
        upper.append(jnp.concatenate([above[:, :LANES], last], axis=1))
    return lower, upper


def predict(count, tracks, unroll):
    def state(load, i):
        cons = load(i)
        prim = primitive(cons)
        speed = sound(prim)
        return prim, speed, (flux_of(prim, cons, 1), cons, jnp.abs(prim[1]) + speed)

    def keep(save_ref, prim, speed, rad_state, rad):
        put_row(save_ref, 0, rad_state[0])
        put_row(save_ref, 1, rad)
        put_row(save_ref, 2, prim)
        save_ref[3, pl.ds(0, NZ), :] = speed
        save_ref[3, pl.ds(NZ, NZ), :] = rad_state[2]

    for load, _, _, save_ref in tracks:
        before = state(load, 0)[2]
        prim, speed, here = state(load, 1)
        keep(save_ref, prim, speed, here, twice_face(*before, *here))

    def one(i, load, faces_at, sink, save_ref):
        cons = load(i)
        low = row_of(save_ref, 1)
        prim = row_of(save_ref, 2)
        speed = save_ref[3, pl.ds(0, NZ), :]
        here = (row_of(save_ref, 0), cons, save_ref[3, pl.ds(NZ, NZ), :])
        next_prim, next_speed, there = state(load, i + 1)
        rad = twice_face(*here, *there)
        keep(save_ref, next_prim, next_speed, there, rad)
        total = [x - y for x, y in zip(rad, low)]
        vert = first_order_faces(prim, cons, speed, 3, 0)
        total = [t + (pltpu.roll(x, NZ - 1, 0) - x) for t, x in zip(total, vert)]
        lower, upper = patched(first_order_faces(prim, cons, speed, 2, 1), *faces_at(i), 1)
        source = added_sources(cons, prim)
        half = []
        for c in range(5):
            value = cons[c] - PRED * (total[c] + (upper[c] - lower[c]))
            half.append(value + 0.5 * step_ratio * source[c] if c in source else value)
        sink(i, primitive(half))

    def step(i, carry):
        for track in tracks:
            one(i, *track)
        return carry

    lax.fori_loop(1, count - 1, step, 0, unroll=unroll)


def correct(count, tracks, unroll):
    def sides(load, i):
        prim = load(i)
        half_slope = [0.5 * minmod(x - a, b - x) for x, a, b in zip(prim, load(i - 1), load(i + 1))]
        return [x - s for x, s in zip(prim, half_slope)], [x + s for x, s in zip(prim, half_slope)]

    for load, *_, save_ref in tracks:
        above = sides(load, 0)[1]
        high, upper_side = sides(load, 1)
        put_row(save_ref, 0, upper_side)
        put_row(save_ref, 1, twice_face(*state_at(above, 1), *state_at(high, 1)))

    def one(i, load, cons_at, faces_ref, group_of, sink, save_ref):
        below = row_of(save_ref, 0)
        low = row_of(save_ref, 1)
        high, upper_side = sides(load, i + 1)
        rad = twice_face(*state_at(below, 1), *state_at(high, 1))
        put_row(save_ref, 0, upper_side)
        put_row(save_ref, 1, rad)
        total = [x - y for x, y in zip(rad, low)]
        prim = load(i)
        vert = second_order_faces(prim, 3, 0)
        total = [t + (pltpu.roll(x, NZ - 1, 0) - x) for t, x in zip(total, vert)]
        lower, upper = patched(second_order_faces(prim, 2, 1), faces_ref, group_of(i), 2)
        source = added_sources(conserved_of(prim), prim)
        cons = cons_at(i)
        done = []
        for c in range(5):
            value = cons[c] - CORR * (total[c] + (upper[c] - lower[c]))
            done.append(value + step_ratio * source[c] if c in source else value)
        sink(i, done)

    def step(i, carry):
        for track in tracks:
            one(i, *track)
        return carry

    lax.fori_loop(1, count - 1, step, 0, unroll=unroll)


def loop_scratch():
    return [
        pltpu.VMEM((8, 5 * NZ, NC), jnp.float32),
        pltpu.VMEM((2, 5 * NZ, LANES), jnp.float32),
        pltpu.VMEM((2, 5 * NZ, LANES), jnp.float32),
    ]


def prep_kernel(x_ref, xt_ref, own_ref):
    for c in range(5):
        xt_ref[:, pl.ds(c * NZ, NZ), :] = jnp.swapaxes(x_ref[pl.ds(c * NZ, NZ)], 0, 1)
    group = lanes_of((5 * NZ, LANES)) // GROUP
    packed = jnp.zeros((5 * NZ, LANES), jnp.float32)
    for row in range(NROW):
        moved = pltpu.roll(xt_ref[row], row * GROUP + GROUP // 2, 1)[:, :LANES]
        packed = jnp.where(group == row, moved, packed)
    own_ref[...] = packed


def rims_kernel(rem_ref, xt_ref, own_ref, paired_ref, crossed_ref, strip_ref, even_ref, odd_ref, end_ref):
    lane = lanes_of((5 * NZ, LANES))
    from_low = (lane % GROUP) < GROUP // 2
    own = own_ref[...]
    even = rem_ref[3] == 0
    low = jnp.where(from_low, jnp.where(even, crossed_ref[...], paired_ref[...]), own)
    high = jnp.where(from_low, own, jnp.where(even, paired_ref[...], crossed_ref[...]))
    strip_ref[:, :LANES] = low
    strip_ref[:, LANES:] = high
    three = WIDTH * GROUP
    lower = jnp.where(lane < three, low, pltpu.roll(high, three, 1))
    upper = jnp.where(lane < three, pltpu.roll(low, three, 1), pltpu.roll(high, 2 * three, 1))
    upward = jnp.bitwise_and(rem_ref[1], 1) == 0
    for ref, flag in ((even_ref, upward), (odd_ref, jnp.logical_not(upward))):
        first = jnp.where(flag, NROW - WIDTH, 0)
        ref[2 * WIDTH] = jnp.where(flag, upper, lower)
        for w in range(WIDTH):
            for side in range(2):
                ref[2 * w + side] = xt_ref[first + w, :, side * LANES : (side + 1) * LANES]

    at_low = rem_ref[1] == 0
    first = jnp.where(at_low, 0, NROW - WIDTH)
    by = jnp.where(at_low, NC - rem_ref[0], rem_ref[0])
    strips = jnp.zeros((5 * NZ, LANES), jnp.float32)
    for w in range(WIDTH):
        row = first + w
        main = xt_ref[row]
        moved = pltpu.roll(main, jnp.bitwise_and(by, NC - 1), 1)
        end_ref[2 * w] = moved[:, :LANES]
        end_ref[2 * w + 1] = moved[:, LANES:]
        above = pltpu.roll(high, jnp.bitwise_and(2 * LANES - GROUP * row - GROUP // 2, LANES - 1), 1)
        below = pltpu.roll(low, jnp.bitwise_and(2 * LANES - GROUP * row - GROUP // 2, LANES - 1), 1)
        wide = jnp.concatenate([main, above, below], axis=1)
        cut = pltpu.roll(wide, jnp.bitwise_and(by - (NC - GROUP // 2) + w * GROUP + 2 * NC, 2 * NC - 1), 1)
        strips = jnp.where(lane // GROUP == w, cut[:, :LANES], strips)
    end_ref[2 * WIDTH] = strips


def inner_kernel(xt_ref, strip_ref, out_ref, kept_ref, prim_ref, save_ref, first_ref, second_ref):
    cons = row_of(strip_ref)
    prim, speed, az = edge_faces_of(cons)
    keep_faces(first_ref, az)
    half = strip_half(cons, prim, speed, az, rolled(cons, GROUP, 1), rolled(cons, -GROUP, 1))
    keep_faces(second_ref, second_order_faces(primitive(half), 2, 1))
    track = (
        lambda i: row_of(xt_ref, i),
        lambda i: (first_ref, i),
        lambda i, arrays: put_row(prim_ref, i, arrays),
        save_ref,
    )
    predict(NROW, [track], 1)
    for n in range(4):
        kept_ref[n] = prim_ref[1 + n]
        kept_ref[4 + n] = prim_ref[NROW - 5 + n]
    track = (
        lambda i: row_of(prim_ref, i + 2),
        lambda i: row_of(xt_ref, i + 2),
        second_ref,
        lambda i: i + 2,
        lambda i, arrays: put_row(out_ref, i + 2, arrays),
        save_ref,
    )
    correct(NROW - 4, [track], 2)


def outer_kernel(
    rem_ref, xt_ref, strip_ref, kept_ref, even_ref, odd_ref, e1_ref, e2_ref, seen_ref, in_ref, whole_ref,
    cons_ref, prim_ref, save_ref, first_ref, second_ref, ghost_ref, strips_ref,
    out_ref, sem,
):
    del seen_ref, in_ref
    rem, rad, last = rem_ref[0], rem_ref[1], rem_ref[2]
    lane = lanes_of((5 * NZ, LANES))
    three = WIDTH * GROUP

    upward = jnp.bitwise_and(rad, 1) == 0

    def from_neighbour(seg, tile):
        flag = upward if seg else jnp.logical_not(upward)
        return jnp.where(flag, even_ref[tile], odd_ref[tile])

    def own_side(seg):
        for w in range(WIDTH):
            for side in range(2):
                cons_ref[seg, WIDTH * seg + w, :, side * LANES : (side + 1) * LANES] = from_neighbour(seg, 2 * w + side)

    def end_side(seg, upper_ref, lower_ref, cut):
        for w in range(WIDTH):
            for side in range(2):
                cons_ref[seg, WIDTH * seg + w, :, side * LANES : (side + 1) * LANES] = jnp.where(
                    lane + side * LANES >= cut, upper_ref[2 * w + side], lower_ref[2 * w + side]
                )

    @pl.when(rad != 0)
    def _():
        own_side(0)
        strips_ref[0] = from_neighbour(0, 2 * WIDTH)
        strips_ref[1] = pltpu.roll(from_neighbour(0, 2 * WIDTH), LANES - three, 1)

    @pl.when(rad == 0)
    def _():
        end_side(0, e1_ref, e2_ref, rem)
        strips_ref[0] = e2_ref[2 * WIDTH]
        strips_ref[1] = e1_ref[2 * WIDTH]

    @pl.when(rad != last)
    def _():
        own_side(1)
        strips_ref[0] = jnp.where(lane < three, strips_ref[0], pltpu.roll(from_neighbour(1, 2 * WIDTH), three, 1))
        strips_ref[1] = jnp.where(lane < three, strips_ref[1], from_neighbour(1, 2 * WIDTH))

    @pl.when(rad == last)
    def _():
        end_side(1, e2_ref, e1_ref, NC - rem)
        strips_ref[0] = jnp.where(lane < three, strips_ref[0], pltpu.roll(e1_ref[2 * WIDTH], three, 1))
        strips_ref[1] = jnp.where(lane < three, strips_ref[1], pltpu.roll(e2_ref[2 * WIDTH], three, 1))

    for w in range(WIDTH):
        cons_ref[0, WIDTH + w] = xt_ref[w]
        cons_ref[1, w] = xt_ref[NROW - WIDTH + w]
    for n in range(4):
        prim_ref[0, 3 + n] = kept_ref[n]
        prim_ref[1, n] = kept_ref[4 + n]

    ghost = [
        jnp.concatenate([strips_ref[0, pl.ds(c * NZ, NZ), :], strips_ref[1, pl.ds(c * NZ, NZ), :]], axis=1)
        for c in range(5)
    ]
    keep_faces(ghost_ref.at[0], edge_faces_of(ghost)[2])
    cons = row_of(strip_ref)
    prim, speed, az = edge_faces_of(cons)
    keep_faces(first_ref, az)
    in_tile = lanes_of((NZ, NC)) % LANES
    below = [
        jnp.where(in_tile < GROUP, a, b) for a, b in zip(rolled(ghost, -2 * GROUP, 1), rolled(cons, GROUP, 1))
    ]
    above = [
        jnp.where(in_tile >= LANES - GROUP, a, b)
        for a, b in zip(rolled(ghost, LANES - 4 * GROUP, 1), rolled(cons, -GROUP, 1))
    ]
    half = strip_half(cons, prim, speed, az, below, above)
    keep_faces(second_ref, second_order_faces(primitive(half), 2, 1))

    group = lanes_of((5 * NZ, LANES)) // GROUP
    for side in range(2):
        mine, both = first_ref[side], ghost_ref[0, side]
        ghost_ref[0, side] = jnp.where(group == 3, pltpu.roll(mine, 3 * GROUP, 1), both)
        ghost_ref[1, side] = jnp.where(group == 1, pltpu.roll(mine, 2 * GROUP, 1), pltpu.roll(both, LANES - GROUP, 1))

    def predicted(seg):
        return (
            lambda i: row_of(cons_ref, seg, i + seg),
            lambda i: (ghost_ref.at[seg], i),
            lambda i, arrays: put_row(prim_ref.at[seg], i - 1 + 4 * seg, arrays),
            save_ref.at[pl.ds(4 * seg, 4)],
        )

    def corrected(seg):
        return (
            lambda i: row_of(prim_ref, seg, i + 1),
            lambda i: row_of(cons_ref, seg, i + 2 - 3 * seg),
            second_ref,
            lambda i: i - 1 + 13 * seg,
            lambda i, arrays: put_row(out_ref.at[seg], i - 1, arrays),
            save_ref.at[pl.ds(4 * seg, 4)],
        )

    predict(5, [predicted(0), predicted(1)], 1)
    correct(5, [corrected(0), corrected(1)], 1)
    copies = [
        pltpu.make_async_copy(out_ref.at[seg], whole_ref.at[pl.ds(seg * (NROW - WIDTH), WIDTH)], sem.at[seg])
        for seg in range(2)
    ]
    for copy in copies:
        copy.start()
    for copy in copies:
        copy.wait()


def remap_kernel(count, turn_ref, x_ref, o_ref):
    shift, frac = turn_ref[0].astype(jnp.int32), turn_ref[1]
    tiles = 2 * count
    hop = jnp.bitwise_and(jnp.right_shift(shift, 7), tiles - 1)
    rem = jnp.bitwise_and(shift, LANES - 1)
    lane = lanes_of((5 * NZ, LANES))
    near, far = lane >= rem, lane > rem
    rest = 1.0 - frac

    def place(k):
        start = pl.multiple_of(jnp.bitwise_and(k, 1) * LANES, LANES)
        return jnp.right_shift(k, 1), slice(None), pl.ds(start, LANES)

    def turned(k):
        tile = x_ref[place(k)]
        return pltpu.roll(tile, rem, 1), pltpu.roll(tile, jnp.bitwise_and(rem + 1, LANES - 1), 1)

    def one(k, before):
        here = turned(k)
        value = rest * jnp.where(near, here[0], before[0]) + frac * jnp.where(far, here[1], before[1])
        o_ref[place(jnp.bitwise_and(k + hop, tiles - 1))] = value
        return here

    lax.fori_loop(0, tiles, one, turned(jnp.int32(tiles - 1)), unroll=8)


def finish_kernel(y_ref, o_ref):
    for c in range(5):
        o_ref[pl.ds(c * NZ, NZ)] = jnp.swapaxes(y_ref[:, pl.ds(c * NZ, NZ), :], 0, 1)


def shape(*dims):
    return jax.ShapeDtypeStruct(dims, jnp.float32)


def local(conserved, shift_cells, shift_frac, boundary_offset):
    azs, rads = lax.axis_size("az"), lax.axis_size("rad")
    az, rad = lax.axis_index("az"), lax.axis_index("rad")
    offset = boundary_offset[0]
    hop, rem = offset // NC, offset % NC
    scalars = jnp.stack([rem, rad, jnp.int32(rads - 1), az % 2]).astype(jnp.int32)
    row_shape, strip_shape = (5 * NZ, NC), (5 * NZ, LANES)
    rows, own = pl.pallas_call(
        prep_kernel,
        out_shape=(shape(NROW, *row_shape), shape(*strip_shape)),
        in_specs=[VMEM],
        out_specs=(VMEM,) * 2,
        compiler_params=PARAMS,
    )(conserved.reshape(5 * NZ, NROW, NC))
    paired = lax.ppermute(own, "az", [(i, i ^ 1) for i in range(azs)])
    crossed = lax.ppermute(own, "az", [(i, (i + 1 if i % 2 else i - 1) % azs) for i in range(azs)])
    rim = shape(2 * WIDTH + 1, *strip_shape)
    strip, even, odd, end = pl.pallas_call(
        rims_kernel,
        out_shape=(shape(*row_shape), rim, rim, rim),
        in_specs=[SMEM] + [VMEM] * 4,
        out_specs=(VMEM,) * 4,
        compiler_params=PARAMS,
    )(scalars, rows, own, paired, crossed)
    row_shift = lax.dynamic_slice_in_dim(shift_cells, az, 1)
    row_frac = lax.dynamic_slice_in_dim(shift_frac, az, 1)
    turn = jnp.concatenate([row_shift.astype(jnp.float32), row_frac])
    strip, turn = lax.optimization_barrier((strip, turn))

    scratch = loop_scratch()

    def inner(rows, strip):
        return pl.pallas_call(
            inner_kernel,
            out_shape=(shape(NROW, *row_shape), shape(8, *row_shape)),
            in_specs=[VMEM] * 2,
            out_specs=(VMEM,) * 2,
            scratch_shapes=[pltpu.VMEM((NROW, *row_shape), jnp.float32), *scratch],
            compiler_params=PARAMS,
            cost_estimate=pl.CostEstimate(flops=30 * 10**6, bytes_accessed=4 * 2**20, transcendentals=0),
        )(rows, strip)

    def ends(k):
        pairs = [(a * rads + rads - 1, (a + k) % azs * rads) for a in range(azs)]
        return pairs + [(b, a) for a, b in pairs]

    def moved_by(k):
        def send(block, even, odd, rows, strip):
            even = lax.ppermute(even, "rad", [(i, i ^ 1) for i in range(rads)])
            odd = lax.ppermute(odd, "rad", [(i, i + 1 if i % 2 else i - 1) for i in range(1, rads - 1)])
            first, second = (lax.ppermute(block, ("az", "rad"), ends(j % azs)) for j in (k, k + 1))
            seen = first[-1, :8] + second[-1, :8]
            return first, second, even, odd, seen, *inner(rows, strip)

        return send

    first, second, even, odd, seen, updated, kept = lax.switch(
        hop, [moved_by(k) for k in range(azs)], end, even, odd, rows, strip
    )
    updated = pl.pallas_call(
        outer_kernel,
        out_shape=shape(NROW, *row_shape),
        in_specs=[SMEM] + [VMEM] * 7 + [ANY] * 2,
        out_specs=ANY,
        input_output_aliases={9: 0},
        scratch_shapes=[
            pltpu.VMEM((2, 6, *row_shape), jnp.float32),
            pltpu.VMEM((2, 7, *row_shape), jnp.float32),
            *scratch,
            pltpu.VMEM((2, 2, *strip_shape), jnp.float32),
            pltpu.VMEM((2, *strip_shape), jnp.float32),
            pltpu.VMEM((2, WIDTH, *row_shape), jnp.float32),
            pltpu.SemaphoreType.DMA((2,)),
        ],
        compiler_params=PARAMS,
    )(scalars, rows, strip, kept, even, odd, first, second, seen, updated)

    whole_row = lax.all_to_all(updated, "az", 0, 0, tiled=True)
    moved = pl.pallas_call(
        functools.partial(remap_kernel, azs),
        out_shape=shape(azs, *row_shape),
        in_specs=[SMEM, VMEM],
        out_specs=VMEM,
        compiler_params=PARAMS,
    )(turn, whole_row)
    back = lax.all_to_all(moved, "az", 0, 0, tiled=True)
    result = pl.pallas_call(
        finish_kernel,
        out_shape=shape(5 * NZ, NROW, NC),
        in_specs=[VMEM],
        out_specs=VMEM,
        compiler_params=PARAMS,
    )(back)
    return result.reshape(5, NZ, NROW, NC)


def solution(mesh):
    in_specs = (P(None, None, "rad", "az"), P("rad"), P("rad"), P())
    out_specs = P(None, None, "rad", "az")
    return jax.shard_map(local, mesh=mesh, in_specs=in_specs, out_specs=out_specs, check_vma=False)
```
